32 devices in a mesh: reg: 8 (over z, y), ep: 4 (over x, core).
Axes of the slice: x: 2, y: 2, z: 4, core: 2. Of those that a mesh axis runs over, the one named last changes fastest.
Arguments:
- log_prices: bfloat16 [32, 64, 256], P('reg', 'ep'), may hold values from -3 to 3
- log_wages: float32 [32, 64], P('reg', 'ep'), may hold values from -12 to 1
- labor_share: float32 [32, 256], P('reg'), may hold values from 0.3 to 0.7
- io_coeffs: bfloat16 [32, 256, 256], P('reg'), may hold values from -0.375 to 0.375
- pair_blocks: bfloat16 [32, 32, 256, 256], P('reg'), may hold values from -0.0201 to 0.801
- log_tau: float32 [32, 32, 256], P('reg'), may hold values from 0.05 to 2
- elasticity: float32 [256], replicated, may hold values from 2 to 40
- partners: int32 [32, 32], replicated, may hold values from 0 to 31, as said below
- list_lengths: int32 [32], replicated, may hold values from 1 to 32, as said below
- price_cotangent: float32 [32, 64, 256], P('reg', 'ep'), may hold values from -6 to 6
Outputs:
- new_prices: bfloat16 [32, 64, 256], P('reg', 'ep')
- price_grad: float32 [32, 64, 256], P('reg', 'ep')
- wage_grad: float32 [32, 64], P('reg', 'ep')
- tau_grad: float32 [32, 32, 256], P('reg')
The draws below stay inside these ranges and needn't reach their ends.
Inputs may be any that keep to these rules, and one draw needn't show every extreme that they name: `partners`: each list names distinct regions. Over their live entries, the 4 importers of an aligned block name at most 16 regions of any one aligned block of 4 regions, and this is reached in every draw. `list_lengths`: in some aligned block of 4 regions every list has 32 live entries.
All inputs are finite; a program needn't handle non-finite values.
Results may differ from the reference program's by a relative error of at most 0.0064.
Values may be sent and summed in bfloat16 or wider, within the bound.
No kernel may reach another device: no remote copies, remote signals or barrier semaphores. Data moves between devices by JAX's collectives and lax.ppermute only.
A program may use at most 64 MiB of HBM per device.

```python
import math
import jax
import jax.numpy as jnp
from jax import lax

J = 256
REG_DEV = 4
LMAX = 32
REGIONS = 32
EPISODES = 64


def draw_log_wages(key, part):
    first_key = jax.random.fold_in(jax.random.fold_in(key, 7), 0)
    return jnp.clip(0.5 * jax.random.normal(first_key, (REGIONS, EPISODES), jnp.float32), -12.0, 1.0)


def draw_pair_blocks(key, part):
    first_key, second_key = jax.random.split(jax.random.fold_in(key, 13), 2)
    shape_full = (REGIONS, LMAX, J, J)
    diagonal = jax.random.uniform(first_key, shape_full, jnp.float32, 0.4, 0.8)
    spread = jax.random.uniform(second_key, shape_full, jnp.float32, -0.02, 0.02)
    rows_index = jax.lax.broadcasted_iota(jnp.int32, shape_full, 2)
    cols_index = jax.lax.broadcasted_iota(jnp.int32, shape_full, 3)
    return jnp.where(rows_index == cols_index, diagonal, spread).astype(jnp.bfloat16)


def draw_partners(key, part):
    blocks = REGIONS // REG_DEV
    first_key, second_key, third_key = jax.random.split(jax.random.fold_in(key, 11), 3)
    ordering = jax.random.randint(first_key, (REGIONS, LMAX), 0, 1 << 20) * LMAX + jnp.arange(LMAX, dtype=jnp.int32)[None, :]
    shuffled = jnp.argsort(ordering, axis=1, stable=True).astype(jnp.int32)
    rotation = jax.random.randint(second_key, (blocks,), 0, blocks)
    inner_shift = jax.random.randint(third_key, (blocks,), 0, REG_DEV)
    region_ids = jnp.arange(REGIONS, dtype=jnp.int32)
    block_ids = region_ids // REG_DEV
    global_slot = shuffled + (region_ids % REG_DEV * LMAX)[:, None]
    source_block = (global_slot + rotation[block_ids][:, None]) % blocks
    inner_index = (global_slot // blocks + inner_shift[block_ids][:, None]) % REG_DEV
    return (source_block * REG_DEV + inner_index).astype(jnp.int32)


def draw_list_lengths(key, part):
    blocks = REGIONS // REG_DEV
    first_key, second_key, third_key = jax.random.split(jax.random.fold_in(key, 23), 3)
    shorter = jax.random.randint(first_key, (REGIONS,), max(LMAX * 3 // 8, 1), LMAX + 1)
    longer = jax.random.randint(second_key, (REGIONS,), 0, 8) == 0
    full_block = jax.random.randint(third_key, (), 0, blocks)
    block_ids = jnp.arange(REGIONS, dtype=jnp.int32) // REG_DEV
    return jnp.where(longer | (block_ids == full_block), LMAX, shorter).astype(jnp.int32)


def level_of(stream_key, dims, shards, smallest, largest):
    gain = 1.0
    for axis_at, shards_of in shards:
        heights = jax.random.uniform(jax.random.fold_in(jax.random.fold_in(stream_key, 6), axis_at), (shards_of,), jnp.float32, smallest / len(shards), largest / len(shards))
        gain = gain * jnp.repeat(jnp.exp(heights), dims[axis_at] // shards_of).reshape((-1,) + (1,) * (len(dims) - 1 - axis_at))
    return gain


def bell_draw(rng, shape, deviation, reach, cuts=(), kind=jnp.bfloat16):
    result = jax.random.normal(rng, shape, jnp.float32) * deviation
    if len(cuts) > 0:
        result = level_of(rng, shape, cuts, -0.22, 0.18) * result
    return jnp.clip(result, min=-reach, max=reach).astype(kind)


def setup_inputs(seed: int = 0) -> dict:
    keys = jax.random.split(jax.random.key(seed), 11)
    log_prices = bell_draw(keys[0], (REGIONS, EPISODES, J), 0.5, 3.0, ((0, 8), (1, 4)))
    log_wages = draw_log_wages(jax.random.fold_in(keys[10], 71), 0)
    labor_share = jnp.clip(0.3 + 0.39999998 * jax.random.uniform(keys[2], (REGIONS, J), jnp.float32) ** level_of(keys[2], (REGIONS, J), ((0, 8),), -0.2, 0.2), 0.3, 0.7)
    io_coeffs = bell_draw(keys[3], (REGIONS, J, J), J ** -0.5, 0.375, ((0, 8),))
    pair_blocks = draw_pair_blocks(jax.random.fold_in(keys[10], 71), 0)
    log_tau = jnp.clip(jnp.exp(math.log(2.0) - 3.6888794 * jax.random.uniform(keys[5], (REGIONS, LMAX, J), jnp.float32) ** level_of(keys[5], (REGIONS, LMAX, J), ((0, 8),), -0.2, 0.2)), 0.05, 2.0)
    elasticity = jnp.clip(jnp.exp(jax.random.uniform(keys[6], (J,), jnp.float32, math.log(2.0), math.log(40.0))), 2.0, 40.0)
    partners = draw_partners(jax.random.fold_in(keys[10], 71), 0)
    list_lengths = draw_list_lengths(jax.random.fold_in(keys[10], 71), 0)
    price_cotangent = bell_draw(keys[9], (REGIONS, EPISODES, J), 1.0, 6.0, ((0, 8), (1, 4)), jnp.float32)
    return {"log_prices": log_prices, "log_wages": log_wages, "labor_share": labor_share, "io_coeffs": io_coeffs, "pair_blocks": pair_blocks, "log_tau": log_tau, "elasticity": elasticity, "partners": partners, "list_lengths": list_lengths, "price_cotangent": price_cotangent}


def reference(log_prices, log_wages, labor_share, io_coeffs, pair_blocks, log_tau, elasticity, partners, list_lengths, price_cotangent):
    combined = labor_share[:, None, :] * log_wages[:, :, None] + jnp.einsum("iek,ikj->iej", log_prices.astype(jnp.float32), io_coeffs.astype(jnp.float32))
    unit_cost = lax.optimization_barrier(combined.astype(jnp.bfloat16))
    slot_index = jnp.arange(LMAX, dtype=jnp.int32)

    def importer(pushed_total, inputs):
        partner_row, length, block, tau_row, cotangent = inputs
        exporter_rows = unit_cost[partner_row].astype(jnp.float32)
        block_wide = block.astype(jnp.float32)
        landed = tau_row[:, None, :] + jnp.einsum("sek,skj->sej", exporter_rows, block_wide)
        live = (slot_index < length)[:, None, None]
        scores = jnp.where(live, -elasticity * landed, -jnp.inf)
        top_score = jnp.max(scores, axis=0)
        weights = jnp.exp(scores - top_score)
        total = jnp.sum(weights, axis=0)
        new_price = -(top_score + jnp.log(total)) / elasticity
        adjoint = cotangent[None] * (weights / total)
        tau_grad = jnp.sum(adjoint, axis=1)
        rounded = lax.optimization_barrier(adjoint.astype(jnp.bfloat16)).astype(jnp.float32)
        pushed = lax.optimization_barrier(jnp.einsum("sej,skj->sek", rounded, block_wide).astype(jnp.bfloat16))
        pushed_wide = jnp.where(live, pushed.astype(jnp.float32), jnp.float32(0.0))
        return pushed_total.at[partner_row].add(pushed_wide), (new_price, tau_grad)

    initial = jnp.zeros((REGIONS, EPISODES, J), jnp.float32)
    cost_adjoint, outputs = lax.scan(importer, initial, (partners, list_lengths, pair_blocks, log_tau, price_cotangent))
    new_prices, tau_grad = outputs
    cost_rounded = lax.optimization_barrier(cost_adjoint.astype(jnp.bfloat16)).astype(jnp.float32)
    price_grad = jnp.einsum("iej,ikj->iek", cost_rounded, io_coeffs.astype(jnp.float32))
    wage_grad = jnp.sum(cost_adjoint * labor_share[:, None, :], axis=2)
    return new_prices.astype(jnp.bfloat16), price_grad, wage_grad, tau_grad
```

```python
import functools

import jax
import jax.numpy as jnp
from jax import lax
from jax.experimental import pallas as pl
from jax.experimental.pallas import tpu as pltpu
from jax.sharding import PartitionSpec as P

F32 = jnp.float32
BF16 = jnp.bfloat16
CONTRACT_LAST = (((1,), (1,)), ((), ()))


def is_power_of_two(n):
    return n & (n - 1) == 0


def peer(i, distance, n):
    return i ^ distance if is_power_of_two(n) else (i + distance) % n


def offset_of(owner, me, n):
    return owner ^ me if is_power_of_two(n) else lax.rem(owner - me + n, n)


def radices(n):
    stages = []
    if n % 2 == 0 and n % 4 == 0 and (n.bit_length() % 2 == 0):
        stages.append(2)
        n //= 2
    while n % 4 == 0 and n > 1:
        stages.append(4)
        n //= 4
    if n > 1:
        stages.append(n)
    return stages


def from_peer(x, distance, axis, n):
    return lax.ppermute(x, axis, [(peer(i, distance, n), i) for i in range(n)])


def to_peer(x, distance, axis, n):
    return lax.ppermute(x, axis, [(i, peer(i, distance, n)) for i in range(n)])


def gather_by_distance(x, axis, n):
    stride = 1
    for radix in radices(n):
        parts = [x] + [from_peer(x, j * stride, axis, n) for j in range(1, radix)]
        x = jnp.concatenate(parts, axis=0)
        stride *= radix
    return x


def scatter_by_distance(x, axis, n):
    stride = n
    for radix in reversed(radices(n)):
        stride //= radix
        blocks = jnp.split(x, radix, axis=0)
        received = [to_peer(blocks[j].astype(BF16), j * stride, axis, n) for j in range(1, radix)]
        x = blocks[0].astype(F32)
        for block in received:
            x = x + block.astype(F32)
    return x


def importers_kernel(
    reg_count,
    me_ref,
    partners_ref,
    lengths_ref,
    costs_ref,
    blocks_ref,
    tau_ref,
    elasticity_ref,
    cotangent_ref,
    prices_ref,
    tau_grad_ref,
    partial_ref,
    weights_ref,
    total_ref,
):
    own, slots, sectors, _ = blocks_ref.shape
    episodes = costs_ref.shape[1]
    me = me_ref[0]
    elasticity = elasticity_ref[...]
    total_ref[...] = jnp.zeros_like(total_ref)
    for r in range(own):
        length = lengths_ref[me * own + r]
        top = jnp.full((episodes, sectors), -jnp.inf, F32)
        places = []
        for s in range(slots):
            partner = partners_ref[me * own + r, s]
            place = offset_of(partner // own, me, reg_count) * own + lax.rem(partner, own)
            places.append(place)
            landed = tau_ref[r, pl.ds(s, 1)] + jnp.dot(
                costs_ref[place], blocks_ref[r, s], preferred_element_type=F32
            )
            score = jnp.where(s < length, -elasticity * landed, -jnp.inf)
            weights_ref[s] = score
            top = jnp.maximum(top, score)
        norm = jnp.zeros((episodes, sectors), F32)
        for s in range(slots):
            weight = jnp.exp(weights_ref[s] - top)
            weights_ref[s] = weight
            norm = norm + weight
        prices_ref[r] = (-(top + jnp.log(norm)) / elasticity).astype(BF16)
        scale = cotangent_ref[r] / norm
        for s in range(slots):
            adjoint = scale * weights_ref[s]
            tau_grad_ref[r, pl.ds(s, 1)] = jnp.sum(adjoint, axis=0, keepdims=True)
            total_ref[places[s]] += lax.dot_general(
                adjoint.astype(BF16), blocks_ref[r, s], CONTRACT_LAST, preferred_element_type=F32
            )
    partial_ref[...] = total_ref[...].astype(BF16)


def shards(
    log_prices,
    log_wages,
    labor_share,
    io_coeffs,
    pair_blocks,
    log_tau,
    elasticity,
    partners,
    list_lengths,
    price_cotangent,
):
    own, episodes, sectors = log_prices.shape
    slots = pair_blocks.shape[1]
    regions = partners.shape[0]
    reg_count = lax.axis_size("reg")
    ep_count = lax.axis_size("ep")
    unit_cost = (
        labor_share[:, None, :] * log_wages[:, :, None]
        + jnp.einsum("iek,ikj->iej", log_prices, io_coeffs, preferred_element_type=F32)
    ).astype(BF16)
    costs = gather_by_distance(unit_cost, "reg", reg_count)
    vmem = pl.BlockSpec(memory_space=pltpu.VMEM)
    smem = pl.BlockSpec(memory_space=pltpu.SMEM)
    new_prices, tau_part, partial = pl.pallas_call(
        functools.partial(importers_kernel, reg_count),
        out_shape=(
            jax.ShapeDtypeStruct((own, episodes, sectors), BF16),
            jax.ShapeDtypeStruct((own, slots, sectors), F32),
            jax.ShapeDtypeStruct((regions, episodes, sectors), BF16),
        ),
        in_specs=[smem, smem, smem, vmem, vmem, vmem, vmem, vmem],
        out_specs=(vmem, vmem, vmem),
        scratch_shapes=[
            pltpu.VMEM((slots, episodes, sectors), F32),
            pltpu.VMEM((regions, episodes, sectors), F32),
        ],
        compiler_params=pltpu.CompilerParams(vmem_limit_bytes=16 << 20),
        name="importers",
    )(
        lax.axis_index("reg").reshape(1),
        partners,
        list_lengths,
        costs,
        pltpu.with_memory_space_constraint(pair_blocks, pltpu.VMEM),
        log_tau,
        elasticity.reshape(1, -1),
        price_cotangent,
    )
    tau_grad = tau_part
    distance = 1
    while distance < ep_count:
        tau_grad = tau_grad + to_peer(tau_grad, distance, "ep", ep_count)
        distance *= 2
    cost_adjoint = scatter_by_distance(partial, "reg", reg_count)
    price_grad = jnp.einsum(
        "iej,ikj->iek", cost_adjoint.astype(BF16), io_coeffs, preferred_element_type=F32
    )
    wage_grad = jnp.sum(cost_adjoint * labor_share[:, None, :], axis=2)
    return new_prices, price_grad, wage_grad, tau_grad


def solution(mesh):
    return jax.shard_map(
        shards,
        mesh=mesh,
        in_specs=(
            P("reg", "ep", None),
            P("reg", "ep"),
            P("reg", None),
            P("reg", None, None),
            P("reg", None, None, None),
            P("reg", None, None),
            P(),
            P(),
            P(),
            P("reg", "ep", None),
        ),
        out_specs=(
            P("reg", "ep", None),
            P("reg", "ep", None),
            P("reg", "ep"),
            P("reg", None, None),
        ),
        check_vma=False,
    )
```

```python
import functools

import jax
import jax.numpy as jnp
from jax import lax
from jax.experimental import pallas as pl
from jax.experimental.pallas import tpu as pltpu
from jax.sharding import PartitionSpec as P

F32 = jnp.float32
BF16 = jnp.bfloat16
CONTRACT_LAST = (((1,), (1,)), ((), ()))
LOWEST = -1e30
VMEM = pl.BlockSpec(memory_space=pltpu.VMEM)
SMEM = pl.BlockSpec(memory_space=pltpu.SMEM)
HBM = pl.BlockSpec(memory_space=pltpu.HBM)


def is_power_of_two(n):
    return n & (n - 1) == 0


def peer(i, distance, n):
    return i ^ distance if is_power_of_two(n) else (i + distance) % n


def distance_of(owner, me, n):
    return owner ^ me if is_power_of_two(n) else lax.rem(owner - me + n, n)


def radices(n):
    stages = []
    if n.bit_length() % 2 == 0 and is_power_of_two(n):
        stages.append(2)
        n //= 2
    while n % 4 == 0:
        stages.append(4)
        n //= 4
    if n > 1 or not stages:
        stages.append(n)
    return stages


def from_peer(x, distance, axis, n):
    return lax.ppermute(x, axis, [(peer(i, distance, n), i) for i in range(n)])


def to_peer(x, distance, axis, n):
    return lax.ppermute(x, axis, [(i, peer(i, distance, n)) for i in range(n)])


def shape(dims, dtype):
    return jax.ShapeDtypeStruct(dims, dtype)


def params(mebibytes):
    return pltpu.CompilerParams(vmem_limit_bytes=mebibytes << 20)


def effort(size):
    return pl.CostEstimate(flops=0, bytes_accessed=size, transcendentals=0)


def in_hbm(x):
    return pltpu.with_memory_space_constraint(x, pltpu.HBM)


class Entries:
    def __init__(self, own, slots, reg_count):
        self.own, self.slots, self.reg_count = own, slots, reg_count
        self.capacity = -(-own * slots // reg_count)
        self.count = self.capacity * reg_count
        self.stride = self.count + 1

    def slot(self, table, entry):
        return table[entry]

    def importer(self, table, entry):
        return table[self.stride + entry]

    def place(self, table, entry):
        return table[2 * self.stride + entry]


def load_kernel(
    entries, me_ref, cost_ref, blocks, tau, cotangent, elasticity, partners, lengths,
    held_ref, tau_ref, cotangent_ref, elasticity_ref, cost_copy_ref, table_ref,
    partners_ref, lengths_ref, found_ref, sems,
):
    own, slots, n, capacity = entries.own, entries.slots, entries.reg_count, entries.capacity
    first = held_ref.shape[0] // 2
    copies = [
        pltpu.make_async_copy(source, target, sems.at[i])
        for i, (source, target) in enumerate(
            (
                (partners, partners_ref),
                (lengths, lengths_ref),
                (tau, tau_ref),
                (cotangent, cotangent_ref),
                (elasticity, elasticity_ref),
                (blocks.at[pl.ds(0, first)], held_ref.at[pl.ds(0, first)]),
            )
        )
    ]
    for copy in copies:
        copy.start()
    cost_copy_ref[...] = cost_ref[...]
    for entry in range(entries.stride):
        table_ref[entry] = 0
        table_ref[entries.stride + entry] = own
        table_ref[2 * entries.stride + entry] = 0
    for distance in range(n):
        found_ref[distance] = 0
    copies[0].wait()
    copies[1].wait()
    me = me_ref[0]
    for r in range(own):
        length = lengths_ref[me * own + r]
        for s in range(slots):
            partner = partners_ref[me * own + r, s]
            distance = distance_of(lax.div(partner, own), me, n)
            found = found_ref[distance]
            entry = jnp.where(s < length, distance * capacity + found, entries.count)
            entry = jnp.minimum(entry, entries.count)
            table_ref[entry] = r * slots + s
            table_ref[entries.stride + entry] = r
            table_ref[2 * entries.stride + entry] = lax.rem(partner, own)
            found_ref[distance] = found + (s < length).astype(jnp.int32)
    for copy in copies[2:]:
        copy.wait()


def score_entries(entries, first, table_ref, costs, held_ref, tau_ref, elasticity_ref, weights_ref, top_ref, norm_ref):
    own, capacity = entries.own, entries.capacity
    scale = -elasticity_ref[...]
    top_ref[...] = jnp.full(top_ref.shape, LOWEST, F32)
    norm_ref[...] = jnp.zeros(norm_ref.shape, F32)
    rows = [(ref, block) for ref in costs for block in range(ref.shape[0] // own)]
    for i in range(weights_ref.shape[0]):
        entry = first * capacity + i
        ref, block = rows[i // capacity]
        slot = entries.slot(table_ref, entry)
        importer = entries.importer(table_ref, entry)
        cost = ref[block * own + entries.place(table_ref, entry)]
        landed = jnp.dot(cost, held_ref[slot], preferred_element_type=F32) + tau_ref[pl.ds(slot, 1)]
        score = scale * landed
        weights_ref[i] = score
        top_ref[importer] = jnp.maximum(top_ref[importer], score)
    for i in range(weights_ref.shape[0]):
        importer = entries.importer(table_ref, first * capacity + i)
        weight = jnp.exp(weights_ref[i] - top_ref[importer])
        weights_ref[i] = weight
        norm_ref[importer] += weight


def near_kernel(entries, n_costs, *refs):
    table_ref, blocks, _, tau_ref, elasticity_ref = refs[:5]
    costs = refs[5 : 5 + n_costs]
    held_ref, weights_ref, top_ref, norm_ref, sem = refs[5 + n_costs :]
    first = held_ref.shape[0] // 2
    rest = held_ref.shape[0] - first
    copy = pltpu.make_async_copy(blocks.at[pl.ds(first, rest)], held_ref.at[pl.ds(first, rest)], sem)
    copy.start()
    copy.wait()
    score_entries(entries, 0, table_ref, costs, held_ref, tau_ref, elasticity_ref, weights_ref, top_ref, norm_ref)


def far_kernel(entries, first, table_ref, held_ref, tau_ref, elasticity_ref, cost_ref, weights_ref, top_ref, norm_ref):
    score_entries(entries, first, table_ref, [cost_ref], held_ref, tau_ref, elasticity_ref, weights_ref, top_ref, norm_ref)


def push_entries(entries, first, table_ref, adjoint_of, held_ref, total_ref):
    total_ref[...] = jnp.zeros(total_ref.shape, F32)
    own, capacity = entries.own, entries.capacity
    for i in range(total_ref.shape[0] // own * capacity):
        entry = first * capacity + i
        place = i // capacity * own + entries.place(table_ref, entry)
        total_ref[place] += lax.dot_general(
            adjoint_of(entry),
            held_ref[entries.slot(table_ref, entry)],
            CONTRACT_LAST,
            preferred_element_type=F32,
        )


def adjoint_kernel(entries, firsts, *refs):
    n = len(firsts)
    table_ref, held_ref, cotangent_ref = refs[:3]
    weights, tops, norms = refs[3 : 3 + n], refs[3 + n : 3 + 2 * n], refs[3 + 2 * n : 3 + 3 * n]
    adjoint_ref, tau_grad_ref, logsum_ref, partial_ref, factor_ref, total_ref = refs[3 + 3 * n :]
    own, capacity = entries.own, entries.capacity
    tau_grad_ref[...] = jnp.zeros(tau_grad_ref.shape, F32)
    for r in range(own):
        top = functools.reduce(jnp.maximum, [ref[r] for ref in tops])
        shrink = [jnp.exp(ref[r] - top) for ref in tops]
        norm = sum(ref[r] * factor for ref, factor in zip(norms, shrink))
        logsum_ref[r] = top + jnp.log(norm)
        scale = cotangent_ref[r] / norm
        for k in range(n):
            factor_ref[k, r] = scale * shrink[k]
    for k in range(n):
        factor_ref[k, own] = jnp.zeros(factor_ref.shape[2:], F32)

    def adjoint(k, i):
        entry = firsts[k] * capacity + i
        value = factor_ref[k, entries.importer(table_ref, entry)] * weights[k][i]
        tau_grad_ref[pl.ds(entries.slot(table_ref, entry), 1)] += jnp.sum(value, axis=0, keepdims=True)
        return value.astype(BF16)

    last = n - 1
    push_entries(
        entries, firsts[last], table_ref, lambda entry: adjoint(last, entry - firsts[last] * capacity), held_ref, total_ref
    )
    partial_ref[...] = total_ref[...].astype(BF16)
    for k in range(last):
        for i in range(weights[k].shape[0]):
            adjoint_ref[firsts[k] * capacity + i] = adjoint(k, i)


def push_kernel(entries, first, table_ref, held_ref, adjoint_ref, partial_ref, total_ref):
    push_entries(entries, first, table_ref, lambda entry: adjoint_ref[entry], held_ref, total_ref)
    partial_ref[...] = total_ref[...].astype(partial_ref.dtype)


def finish_kernel(
    own_sum_ref, received_ref, io_ref, share_ref, logsum_ref, elasticity_ref, prices_ref, price_grad_ref, wage_grad_ref
):
    for r in range(own_sum_ref.shape[0]):
        cost_adjoint = own_sum_ref[r] + received_ref[r].astype(F32)
        price_grad_ref[r] = lax.dot_general(
            cost_adjoint.astype(BF16), io_ref[r], CONTRACT_LAST, preferred_element_type=F32
        )
        wage_grad_ref[r] = jnp.sum(cost_adjoint * share_ref[pl.ds(r, 1)], axis=1)
        prices_ref[r] = (-logsum_ref[r] / elasticity_ref[...]).astype(BF16)


def shards(
    log_prices,
    log_wages,
    labor_share,
    io_coeffs,
    pair_blocks,
    log_tau,
    elasticity,
    partners,
    list_lengths,
    price_cotangent,
):
    own, episodes, sectors = log_prices.shape
    slots = pair_blocks.shape[1]
    reg_count = lax.axis_size("reg")
    ep_count = lax.axis_size("ep")
    entries = Entries(own, slots, reg_count)
    blocks = pair_blocks.reshape(own * slots, sectors, sectors)
    row = (episodes, sectors)
    stages = radices(reg_count)
    last_radix = stages[-1]
    last_stride = reg_count // last_radix
    capacity = entries.capacity

    unit_cost = (
        labor_share[:, None, :] * log_wages[:, :, None]
        + jnp.einsum("iek,ikj->iej", log_prices, io_coeffs, preferred_element_type=F32)
    ).astype(BF16)

    held, tau, cotangent, elastic, cost_copy, table = pl.pallas_call(
        functools.partial(load_kernel, entries),
        out_shape=(
            shape(blocks.shape, BF16),
            shape((own * slots, sectors), F32),
            shape(price_cotangent.shape, F32),
            shape((1, sectors), F32),
            shape(unit_cost.shape, BF16),
            pltpu.SMEM((3 * entries.stride,), jnp.int32),
        ),
        in_specs=[SMEM, VMEM] + [HBM] * 6,
        out_specs=(VMEM,) * 5 + (SMEM,),
        scratch_shapes=[
            pltpu.SMEM(partners.shape, jnp.int32),
            pltpu.SMEM(list_lengths.shape, jnp.int32),
            pltpu.SMEM((reg_count,), jnp.int32),
            pltpu.SemaphoreType.DMA((6,)),
        ],
        compiler_params=params(1),
        cost_estimate=effort(blocks.size),
        name="load",
    )(
        lax.axis_index("reg").reshape(1),
        unit_cost,
        in_hbm(blocks),
        in_hbm(log_tau.reshape(own * slots, sectors)),
        in_hbm(price_cotangent),
        in_hbm(elasticity.reshape(1, sectors)),
        in_hbm(partners),
        in_hbm(list_lengths),
    )

    near = [unit_cost]
    stride = 1
    for radix in stages[:-1]:
        if stride > 1:
            near[0] = cost_copy
        whole = jnp.concatenate(near, axis=0)
        near += [from_peer(whole, j * stride, "reg", reg_count) for j in range(1, radix)]
        stride *= radix
    near[0] = cost_copy
    whole = jnp.concatenate(near, axis=0)
    far = [from_peer(whole, j * stride, "reg", reg_count) for j in range(1, last_radix)]

    def scored(count):
        return (
            shape((count,) + row, F32),
            shape((own + 1,) + row, F32),
            shape((own + 1,) + row, F32),
        )

    piece = last_stride * capacity
    held, *near_scores = pl.pallas_call(
        functools.partial(near_kernel, entries, len(near)),
        out_shape=(shape(blocks.shape, BF16),) + scored(piece),
        in_specs=[SMEM, HBM] + [VMEM] * (3 + len(near)),
        out_specs=(VMEM,) * 4,
        scratch_shapes=[pltpu.SemaphoreType.DMA],
        input_output_aliases={2: 0},
        compiler_params=params(2),
        cost_estimate=effort(blocks.size),
        name="near",
    )(table, in_hbm(blocks), held, tau, elastic, *near)
    scores = [near_scores]
    for j, cost in enumerate(far, 1):
        scores.append(
            pl.pallas_call(
                functools.partial(far_kernel, entries, j * last_stride),
                out_shape=scored(piece),
                in_specs=[SMEM] + [VMEM] * 4,
                out_specs=(VMEM,) * 3,
                compiler_params=params(2),
                cost_estimate=effort(blocks.size // last_radix * 2),
                name="far",
            )(table, held, tau, elastic, cost)
        )
    firsts = [j * last_stride for j in range(last_radix)]
    partial_dims = (last_stride * own,) + row
    adjoint, tau_grad, logsum, partial = pl.pallas_call(
        functools.partial(adjoint_kernel, entries, firsts),
        out_shape=(
            shape((max(entries.count - piece, 1),) + row, BF16),
            shape((own * slots, sectors), F32),
            shape((own,) + row, F32),
            shape(partial_dims, BF16),
        ),
        in_specs=[SMEM] + [VMEM] * (2 + 3 * last_radix),
        out_specs=(VMEM,) * 4,
        scratch_shapes=[
            pltpu.VMEM((last_radix, own + 1) + row, F32),
            pltpu.VMEM(partial_dims, F32),
        ],
        compiler_params=params(8),
        cost_estimate=effort(blocks.size // last_radix * 2),
        name="adjoint",
    )(table, held, cotangent, *[s[0] for s in scores], *[s[1] for s in scores], *[s[2] for s in scores])

    def push(j, dtype):
        return pl.pallas_call(
            functools.partial(push_kernel, entries, firsts[j]),
            out_shape=shape(partial_dims, dtype),
            in_specs=[SMEM, VMEM, VMEM],
            out_specs=VMEM,
            scratch_shapes=[pltpu.VMEM(partial_dims, F32)],
            compiler_params=params(8),
            cost_estimate=effort(blocks.size // last_radix * 2),
            name="push",
        )(table, held, adjoint)

    received = [to_peer(partial, firsts[-1], "reg", reg_count)]
    for j in range(last_radix - 2, 0, -1):
        received.append(to_peer(push(j, BF16), firsts[j], "reg", reg_count))
    summed = push(0, F32)
    for block in received:
        summed = summed + block.astype(F32)
    stride = last_stride
    arrived = jnp.zeros((own,) + row, BF16)
    for radix in reversed(stages[:-1]):
        stride //= radix
        parts = jnp.split(summed, radix, axis=0)
        received = [to_peer(parts[j].astype(BF16), j * stride, "reg", reg_count) for j in range(1, radix)]
        summed = parts[0]
        if stride == 1:
            arrived = received.pop()
        for block in received:
            summed = summed + block.astype(F32)

    if is_power_of_two(ep_count):
        distance = 1
        while distance < ep_count:
            tau_grad = tau_grad + to_peer(tau_grad, distance, "ep", ep_count)
            distance *= 2
    else:
        tau_grad = lax.psum(tau_grad, "ep")

    new_prices, price_grad, wage_grad = pl.pallas_call(
        finish_kernel,
        out_shape=(shape((own,) + row, BF16), shape((own,) + row, F32), shape((own, episodes), F32)),
        in_specs=[VMEM] * 6,
        out_specs=(VMEM,) * 3,
        compiler_params=params(4),
        name="finish",
    )(summed, arrived, io_coeffs, labor_share, logsum, elastic)
    return new_prices, price_grad, wage_grad, tau_grad.reshape(own, slots, sectors)


def solution(mesh):
    return jax.shard_map(
        shards,
        mesh=mesh,
        in_specs=(
            P("reg", "ep", None),
            P("reg", "ep"),
            P("reg", None),
            P("reg", None, None),
            P("reg", None, None, None),
            P("reg", None, None),
            P(),
            P(),
            P(),
            P("reg", "ep", None),
        ),
        out_specs=(
            P("reg", "ep", None),
            P("reg", "ep", None),
            P("reg", "ep"),
            P("reg", None, None),
        ),
        check_vma=False,
    )
```

```python
import functools

import jax
import jax.numpy as jnp
from jax import lax
from jax.experimental import pallas as pl
from jax.experimental.pallas import tpu as pltpu
from jax.sharding import PartitionSpec as P

F32 = jnp.float32
BF16 = jnp.bfloat16
CONTRACT_LAST = (((1,), (1,)), ((), ()))
LOWEST = -1e30
VMEM = pl.BlockSpec(memory_space=pltpu.VMEM)
SMEM = pl.BlockSpec(memory_space=pltpu.SMEM)
HBM = pl.BlockSpec(memory_space=pltpu.HBM)


def is_power_of_two(n):
    return n & (n - 1) == 0


def peer(i, distance, n):
    return i ^ distance if is_power_of_two(n) else (i + distance) % n


def distance_of(owner, me, n):
    return owner ^ me if is_power_of_two(n) else lax.rem(owner - me + n, n)


def radices(n):
    stages = []
    if n.bit_length() % 2 == 0 and is_power_of_two(n):
        stages.append(2)
        n //= 2
    while n % 4 == 0:
        stages.append(4)
        n //= 4
    if n > 1 or not stages:
        stages.append(n)
    return stages


def from_peer(x, distance, axis, n):
    return lax.ppermute(x, axis, [(peer(i, distance, n), i) for i in range(n)])


def to_peer(x, distance, axis, n):
    return lax.ppermute(x, axis, [(i, peer(i, distance, n)) for i in range(n)])


def shape(dims, dtype):
    return jax.ShapeDtypeStruct(dims, dtype)


def params(mebibytes):
    return pltpu.CompilerParams(vmem_limit_bytes=mebibytes << 20)


def effort(size):
    return pl.CostEstimate(flops=0, bytes_accessed=size, transcendentals=0)


def in_hbm(x):
    return pltpu.with_memory_space_constraint(x, pltpu.HBM)


class Entries:
    def __init__(self, own, slots, reg_count):
        self.own, self.slots, self.reg_count = own, slots, reg_count
        self.capacity = -(-own * slots // reg_count)
        self.count = self.capacity * reg_count
        self.stride = self.count + 1

    def slot(self, table, entry):
        return table[entry]

    def importer(self, table, entry):
        return table[self.stride + entry]

    def place(self, table, entry):
        return table[2 * self.stride + entry]


def load_kernel(
    entries, me_ref, cost_ref, blocks, tau, cotangent, elasticity, partners, lengths,
    held_ref, tau_ref, cotangent_ref, elasticity_ref, cost_copy_ref, table_ref,
    partners_ref, lengths_ref, found_ref, sems,
):
    own, slots, n, capacity = entries.own, entries.slots, entries.reg_count, entries.capacity
    first = held_ref.shape[0] // 2
    copies = [
        pltpu.make_async_copy(source, target, sems.at[i])
        for i, (source, target) in enumerate(
            (
                (partners, partners_ref),
                (lengths, lengths_ref),
                (tau, tau_ref),
                (cotangent, cotangent_ref),
                (elasticity, elasticity_ref),
                (blocks.at[pl.ds(0, first)], held_ref.at[pl.ds(0, first)]),
            )
        )
    ]
    for copy in copies:
        copy.start()
    cost_copy_ref[...] = cost_ref[...]
    for entry in range(entries.stride):
        table_ref[entry] = 0
        table_ref[entries.stride + entry] = own
        table_ref[2 * entries.stride + entry] = 0
    for distance in range(n):
        found_ref[distance] = 0
    copies[0].wait()
    copies[1].wait()
    me = me_ref[0]
    for r in range(own):
        length = lengths_ref[me * own + r]
        for s in range(slots):
            partner = partners_ref[me * own + r, s]
            distance = distance_of(lax.div(partner, own), me, n)
            found = found_ref[distance]
            entry = jnp.where(s < length, distance * capacity + found, entries.count)
            entry = jnp.minimum(entry, entries.count)
            table_ref[entry] = r * slots + s
            table_ref[entries.stride + entry] = r
            table_ref[2 * entries.stride + entry] = lax.rem(partner, own)
            found_ref[distance] = found + (s < length).astype(jnp.int32)
    for copy in copies[2:]:
        copy.wait()


def score_entries(entries, first, table_ref, costs, held_ref, tau_ref, elasticity_ref, weights_ref, top_ref, norm_ref):
    own, capacity = entries.own, entries.capacity
    scale = -elasticity_ref[...]
    top_ref[...] = jnp.full(top_ref.shape, LOWEST, F32)
    norm_ref[...] = jnp.zeros(norm_ref.shape, F32)
    rows = [(ref, block) for ref in costs for block in range(ref.shape[0] // own)]
    for i in range(weights_ref.shape[0]):
        entry = first * capacity + i
        ref, block = rows[i // capacity]
        slot = entries.slot(table_ref, entry)
        importer = entries.importer(table_ref, entry)
        cost = ref[block * own + entries.place(table_ref, entry)]
        landed = jnp.dot(cost, held_ref[slot], preferred_element_type=F32) + tau_ref[pl.ds(slot, 1)]
        score = scale * landed
        weights_ref[i] = score
        top_ref[importer] = jnp.maximum(top_ref[importer], score)
    for i in range(weights_ref.shape[0]):
        importer = entries.importer(table_ref, first * capacity + i)
        weight = jnp.exp(weights_ref[i] - top_ref[importer])
        weights_ref[i] = weight
        norm_ref[importer] += weight


def near_kernel(entries, n_costs, *refs):
    table_ref, blocks, _, tau_ref, elasticity_ref = refs[:5]
    costs = refs[5 : 5 + n_costs]
    held_ref, weights_ref, top_ref, norm_ref, sem = refs[5 + n_costs :]
    first = held_ref.shape[0] // 2
    rest = held_ref.shape[0] - first
    copy = pltpu.make_async_copy(blocks.at[pl.ds(first, rest)], held_ref.at[pl.ds(first, rest)], sem)
    copy.start()
    copy.wait()
    score_entries(entries, 0, table_ref, costs, held_ref, tau_ref, elasticity_ref, weights_ref, top_ref, norm_ref)


def far_kernel(entries, first, table_ref, held_ref, tau_ref, elasticity_ref, cost_ref, weights_ref, top_ref, norm_ref):
    score_entries(entries, first, table_ref, [cost_ref], held_ref, tau_ref, elasticity_ref, weights_ref, top_ref, norm_ref)


def push_entries(entries, distances, table_ref, adjoint_of, held_ref, total_ref):
    total_ref[...] = jnp.zeros(total_ref.shape, F32)
    for block, distance in enumerate(distances):
        for entry in range(distance * entries.capacity, (distance + 1) * entries.capacity):
            total_ref[block * entries.own + entries.place(table_ref, entry)] += lax.dot_general(
                adjoint_of(entry),
                held_ref[entries.slot(table_ref, entry)],
                CONTRACT_LAST,
                preferred_element_type=F32,
            )


def adjoint_kernel(entries, n, distances, *refs):
    table_ref, held_ref, cotangent_ref = refs[:3]
    weights, tops, norms = refs[3 : 3 + n], refs[3 + n : 3 + 2 * n], refs[3 + 2 * n : 3 + 3 * n]
    adjoint_ref, tau_grad_ref, logsum_ref, partial_ref, factor_ref, total_ref = refs[3 + 3 * n :]
    own, capacity = entries.own, entries.capacity
    piece = weights[0].shape[0]
    tau_grad_ref[...] = jnp.zeros(tau_grad_ref.shape, F32)
    for r in range(own):
        top = functools.reduce(jnp.maximum, [ref[r] for ref in tops])
        shrink = [jnp.exp(ref[r] - top) for ref in tops]
        norm = sum(ref[r] * factor for ref, factor in zip(norms, shrink))
        logsum_ref[r] = top + jnp.log(norm)
        scale = cotangent_ref[r] / norm
        for k in range(n):
            factor_ref[k, r] = scale * shrink[k]
    for k in range(n):
        factor_ref[k, own] = jnp.zeros(factor_ref.shape[2:], F32)

    def adjoint(entry):
        k, i = divmod(entry, piece)
        value = factor_ref[k, entries.importer(table_ref, entry)] * weights[k][i]
        tau_grad_ref[pl.ds(entries.slot(table_ref, entry), 1)] += jnp.sum(value, axis=0, keepdims=True)
        return value.astype(BF16)

    push_entries(entries, distances, table_ref, adjoint, held_ref, total_ref)
    partial_ref[...] = total_ref[...].astype(BF16)
    for entry in range(entries.count):
        if entry // capacity not in distances:
            adjoint_ref[entry] = adjoint(entry)


def push_kernel(entries, distances, table_ref, held_ref, adjoint_ref, partial_ref, total_ref):
    push_entries(entries, distances, table_ref, lambda entry: adjoint_ref[entry], held_ref, total_ref)
    partial_ref[...] = total_ref[...].astype(partial_ref.dtype)


def finish_kernel(n, *refs):
    own_sum_ref, received = refs[0], refs[1 : 1 + n]
    io_ref, share_ref, logsum_ref, elasticity_ref, tau_ref, tau_received_ref = refs[1 + n : 7 + n]
    prices_ref, price_grad_ref, wage_grad_ref, tau_grad_ref = refs[7 + n :]
    tau_grad_ref[...] = tau_ref[...] + tau_received_ref[...]
    for r in range(own_sum_ref.shape[0]):
        prices_ref[r] = (-logsum_ref[r] / elasticity_ref[...]).astype(BF16)
        cost_adjoint = own_sum_ref[r]
        for ref in received:
            cost_adjoint = cost_adjoint + ref[r].astype(F32)
        price_grad_ref[r] = lax.dot_general(
            cost_adjoint.astype(BF16), io_ref[r], CONTRACT_LAST, preferred_element_type=F32
        )
        wage_grad_ref[r] = jnp.sum(cost_adjoint * share_ref[pl.ds(r, 1)], axis=1)


def shards(
    log_prices,
    log_wages,
    labor_share,
    io_coeffs,
    pair_blocks,
    log_tau,
    elasticity,
    partners,
    list_lengths,
    price_cotangent,
):
    own, episodes, sectors = log_prices.shape
    slots = pair_blocks.shape[1]
    reg_count = lax.axis_size("reg")
    ep_count = lax.axis_size("ep")
    entries = Entries(own, slots, reg_count)
    blocks = pair_blocks.reshape(own * slots, sectors, sectors)
    row = (episodes, sectors)
    stages = radices(reg_count)
    last_radix = stages[-1]
    last_stride = reg_count // last_radix
    capacity = entries.capacity

    unit_cost = (
        labor_share[:, None, :] * log_wages[:, :, None]
        + jnp.einsum("iek,ikj->iej", log_prices, io_coeffs, preferred_element_type=F32)
    ).astype(BF16)

    held, tau, cotangent, elastic, cost_copy, table = pl.pallas_call(
        functools.partial(load_kernel, entries),
        out_shape=(
            shape(blocks.shape, BF16),
            shape((own * slots, sectors), F32),
            shape(price_cotangent.shape, F32),
            shape((1, sectors), F32),
            shape(unit_cost.shape, BF16),
            pltpu.SMEM((3 * entries.stride,), jnp.int32),
        ),
        in_specs=[SMEM, VMEM] + [HBM] * 6,
        out_specs=(VMEM,) * 5 + (SMEM,),
        scratch_shapes=[
            pltpu.SMEM(partners.shape, jnp.int32),
            pltpu.SMEM(list_lengths.shape, jnp.int32),
            pltpu.SMEM((reg_count,), jnp.int32),
            pltpu.SemaphoreType.DMA((6,)),
        ],
        compiler_params=params(1),
        cost_estimate=effort(blocks.size),
        name="load",
    )(
        lax.axis_index("reg").reshape(1),
        unit_cost,
        in_hbm(blocks),
        in_hbm(log_tau.reshape(own * slots, sectors)),
        in_hbm(price_cotangent),
        in_hbm(elasticity.reshape(1, sectors)),
        in_hbm(partners),
        in_hbm(list_lengths),
    )

    near = [unit_cost]
    stride = 1
    for radix in stages[:-1]:
        if stride > 1:
            near[0] = cost_copy
        whole = jnp.concatenate(near, axis=0)
        near += [from_peer(whole, j * stride, "reg", reg_count) for j in range(1, radix)]
        stride *= radix
    near[0] = cost_copy
    whole = jnp.concatenate(near, axis=0)
    far = [from_peer(whole, j * stride, "reg", reg_count) for j in range(1, last_radix)]

    def scored(count):
        return (
            shape((count,) + row, F32),
            shape((own + 1,) + row, F32),
            shape((own + 1,) + row, F32),
        )

    piece = last_stride * capacity
    held, *near_scores = pl.pallas_call(
        functools.partial(near_kernel, entries, len(near)),
        out_shape=(shape(blocks.shape, BF16),) + scored(piece),
        in_specs=[SMEM, HBM] + [VMEM] * (3 + len(near)),
        out_specs=(VMEM,) * 4,
        scratch_shapes=[pltpu.SemaphoreType.DMA],
        input_output_aliases={2: 0},
        compiler_params=params(2),
        cost_estimate=effort(blocks.size),
        name="near",
    )(table, in_hbm(blocks), held, tau, elastic, *near)
    scores = [near_scores]
    for j, cost in enumerate(far, 1):
        scores.append(
            pl.pallas_call(
                functools.partial(far_kernel, entries, j * last_stride),
                out_shape=scored(piece),
                in_specs=[SMEM] + [VMEM] * 4,
                out_specs=(VMEM,) * 3,
                compiler_params=params(2),
                cost_estimate=effort(blocks.size // last_radix * 2),
                name="far",
            )(table, held, tau, elastic, cost)
        )
    radix = stages[0]
    groups = [range(j, reg_count, radix) for j in range(radix)]
    partial_dims = (reg_count // radix * own,) + row
    adjoint, tau_grad, logsum, partial = pl.pallas_call(
        functools.partial(adjoint_kernel, entries, last_radix, groups[-1]),
        out_shape=(
            shape((entries.count,) + row, BF16),
            shape((own * slots, sectors), F32),
            shape((own,) + row, F32),
            shape(partial_dims, BF16),
        ),
        in_specs=[SMEM] + [VMEM] * (2 + 3 * last_radix),
        out_specs=(VMEM,) * 4,
        scratch_shapes=[
            pltpu.VMEM((last_radix, own + 1) + row, F32),
            pltpu.VMEM(partial_dims, F32),
        ],
        compiler_params=params(8),
        cost_estimate=effort(blocks.size),
        name="adjoint",
    )(table, held, cotangent, *[s[0] for s in scores], *[s[1] for s in scores], *[s[2] for s in scores])

    def push(j, dtype):
        return pl.pallas_call(
            functools.partial(push_kernel, entries, groups[j]),
            out_shape=shape(partial_dims, dtype),
            in_specs=[SMEM, VMEM, VMEM],
            out_specs=VMEM,
            scratch_shapes=[pltpu.VMEM(partial_dims, F32)],
            compiler_params=params(8),
            cost_estimate=effort(blocks.size),
            name="push",
        )(table, held, adjoint)

    received = [to_peer(partial, radix - 1, "reg", reg_count)] if radix > 1 else []
    for j in range(radix - 2, 0, -1):
        received.append(to_peer(push(j, BF16), j, "reg", reg_count))
    summed = push(0, F32) if radix > 1 else partial.astype(F32)
    stride = 1
    for following in stages[1:]:
        for block in received:
            summed = summed + block.astype(F32)
        stride *= radix
        radix = following
        parts = summed.reshape((-1, radix, own) + row)
        received = [
            to_peer(parts[:, j].reshape((-1,) + row).astype(BF16), j * stride, "reg", reg_count)
            for j in range(radix - 1, 0, -1)
        ]
        summed = parts[:, 0].reshape((-1,) + row)

    if is_power_of_two(ep_count):
        tau_received = jnp.zeros_like(tau_grad)
        distance = 1
        while distance < ep_count:
            tau_grad = tau_grad + tau_received if distance > 1 else tau_grad
            tau_received = to_peer(tau_grad, distance, "ep", ep_count)
            distance *= 2
    else:
        tau_grad = lax.psum(tau_grad, "ep")
        tau_received = jnp.zeros_like(tau_grad)

    new_prices, price_grad, wage_grad, tau_grad = pl.pallas_call(
        functools.partial(finish_kernel, len(received)),
        out_shape=(
            shape((own,) + row, BF16),
            shape((own,) + row, F32),
            shape((own, episodes), F32),
            shape(tau_grad.shape, F32),
        ),
        in_specs=[VMEM] * (7 + len(received)),
        out_specs=(VMEM,) * 4,
        compiler_params=params(4),
        name="finish",
    )(summed, *received, io_coeffs, labor_share, logsum, elastic, tau_grad, tau_received)
    return new_prices, price_grad, wage_grad, tau_grad.reshape(own, slots, sectors)


def solution(mesh):
    return jax.shard_map(
        shards,
        mesh=mesh,
        in_specs=(
            P("reg", "ep", None),
            P("reg", "ep"),
            P("reg", None),
            P("reg", None, None),
            P("reg", None, None, None),
            P("reg", None, None),
            P(),
            P(),
            P(),
            P("reg", "ep", None),
        ),
        out_specs=(
            P("reg", "ep", None),
            P("reg", "ep", None),
            P("reg", "ep"),
            P("reg", None, None),
        ),
        check_vma=False,
    )
```

```python
import functools

import jax
import jax.numpy as jnp
from jax import lax
from jax.experimental import pallas as pl
from jax.experimental.pallas import tpu as pltpu
from jax.sharding import PartitionSpec as P

F32 = jnp.float32
BF16 = jnp.bfloat16
CONTRACT_LAST = (((1,), (1,)), ((), ()))
LOWEST = -1e30
VMEM = pl.BlockSpec(memory_space=pltpu.VMEM)
SMEM = pl.BlockSpec(memory_space=pltpu.SMEM)
HBM = pl.BlockSpec(memory_space=pltpu.HBM)


def is_power_of_two(n):
    return n & (n - 1) == 0


def peer(i, distance, n):
    return i ^ distance if is_power_of_two(n) else (i + distance) % n


def distance_of(owner, me, n):
    return owner ^ me if is_power_of_two(n) else lax.rem(owner - me + n, n)


def radices(n):
    stages = []
    if n.bit_length() % 2 == 0 and is_power_of_two(n):
        stages.append(2)
        n //= 2
    while n % 4 == 0:
        stages.append(4)
        n //= 4
    if n > 1 or not stages:
        stages.append(n)
    return stages


def from_peer(x, distance, axis, n):
    return lax.ppermute(x, axis, [(peer(i, distance, n), i) for i in range(n)])


def to_peer(x, distance, axis, n):
    return lax.ppermute(x, axis, [(i, peer(i, distance, n)) for i in range(n)])


def shape(dims, dtype):
    return jax.ShapeDtypeStruct(dims, dtype)


def params(mebibytes):
    return pltpu.CompilerParams(vmem_limit_bytes=mebibytes << 20)


def effort(size):
    return pl.CostEstimate(flops=0, bytes_accessed=size, transcendentals=0)


def in_hbm(x):
    return pltpu.with_memory_space_constraint(x, pltpu.HBM)


class Entries:
    def __init__(self, own, slots, reg_count):
        self.own, self.slots, self.reg_count = own, slots, reg_count
        self.slot_count = own * slots
        self.dense = reg_count * own <= slots
        self.capacity = own * own if self.dense else -(-own * slots // reg_count)
        self.count = self.capacity * reg_count
        self.stride = self.count + 1
        self.columns = 2 if self.dense else 4

    def slot(self, table, entry):
        return table[entry]

    def row(self, table, entry):
        return table[self.stride + entry]

    def live(self, table, entry):
        return self.row(table, entry) < self.slot_count

    def importer(self, table, entry):
        return entry % self.capacity // self.own if self.dense else table[2 * self.stride + entry]

    def place(self, table, entry):
        return entry % self.own if self.dense else table[3 * self.stride + entry]

    def fill(self, table, found, partners, lengths, me):
        own = self.own
        for entry in range(self.stride):
            for column, value in enumerate((0, self.slot_count, own, 0)[: self.columns]):
                table[column * self.stride + entry] = value
        if not self.dense:
            for distance in range(self.reg_count):
                found[distance] = 0
        for r in range(own):
            length = lengths[me * own + r]
            for s in range(self.slots):
                partner = partners[me * own + r, s]
                distance = distance_of(lax.div(partner, own), me, self.reg_count)
                place = lax.rem(partner, own)
                slot = r * self.slots + s
                if self.dense:
                    entry = distance * self.capacity + r * own + place
                    columns = (slot, slot)
                else:
                    entry = distance * self.capacity + found[distance]
                    columns = (slot, slot, r, place)
                    found[distance] += (s < length).astype(jnp.int32)
                entry = jnp.minimum(jnp.where(s < length, entry, self.count), self.count)
                for column, value in enumerate(columns):
                    table[column * self.stride + entry] = value


def load_kernel(
    entries, me_ref, cost_ref, blocks, tau, cotangent, elasticity, partners, lengths,
    held_ref, tau_ref, cotangent_ref, elasticity_ref, cost_copy_ref, table_ref,
    partners_ref, lengths_ref, found_ref, sems,
):
    copies = [
        pltpu.make_async_copy(source, target, sems.at[i])
        for i, (source, target) in enumerate(
            (
                (partners, partners_ref),
                (lengths, lengths_ref),
                (tau, tau_ref),
                (cotangent, cotangent_ref),
                (elasticity, elasticity_ref),
                (blocks.at[pl.ds(0, entries.slots)], held_ref.at[pl.ds(0, entries.slots)]),
            )
        )
    ]
    for copy in copies:
        copy.start()
    cost_copy_ref[...] = cost_ref[...]
    copies[0].wait()
    copies[1].wait()
    entries.fill(table_ref, found_ref, partners_ref, lengths_ref, me_ref[0])
    for copy in copies[2:]:
        copy.wait()


def score_entries(
    entries, first, table_ref, costs, held_ref, tau_ref, elasticity_ref, weights_ref, top_ref, norm_ref, arrive=lambda r: None
):
    own, capacity = entries.own, entries.capacity
    count = weights_ref.shape[0]
    scale = -elasticity_ref[...]
    lowest = jnp.full(top_ref.shape[1:], LOWEST, F32)
    zero = jnp.zeros(top_ref.shape[1:], F32)
    rows = [(ref, block) for ref in costs for block in range(ref.shape[0] // own)]

    def score(i):
        entry = first * capacity + i
        ref, block = rows[i // capacity]
        slot = entries.slot(table_ref, entry)
        cost = ref[block * own + entries.place(table_ref, entry)]
        landed = jnp.dot(cost, held_ref[slot], preferred_element_type=F32) + tau_ref[pl.ds(slot, 1)]
        return scale * landed

    if entries.dense:
        for r in range(own):
            arrive(r)
            members = [i for i in range(count) if entries.importer(table_ref, i) == r]
            scores = [jnp.where(entries.live(table_ref, first * capacity + i), score(i), -jnp.inf) for i in members]
            top = functools.reduce(jnp.maximum, scores, lowest)
            norm = zero
            for i, value in zip(members, scores):
                weight = jnp.exp(value - top)
                weights_ref[i] = weight
                norm = norm + weight
            top_ref[r] = top
            norm_ref[r] = norm
        return
    arrive(None)
    top_ref[...] = jnp.full(top_ref.shape, LOWEST, F32)
    norm_ref[...] = jnp.zeros(norm_ref.shape, F32)
    for i in range(count):
        importer = entries.importer(table_ref, first * capacity + i)
        value = score(i)
        weights_ref[i] = value
        top_ref[importer] = jnp.maximum(top_ref[importer], value)
    for i in range(count):
        importer = entries.importer(table_ref, first * capacity + i)
        weight = jnp.exp(weights_ref[i] - top_ref[importer])
        weights_ref[i] = weight
        norm_ref[importer] += weight


def near_kernel(entries, n_costs, *refs):
    table_ref, blocks, _, tau_ref, elasticity_ref = refs[:5]
    costs = refs[5 : 5 + n_costs]
    held_ref, weights_ref, top_ref, norm_ref, sems = refs[5 + n_costs :]
    own, slots = entries.own, entries.slots
    copies = [
        pltpu.make_async_copy(blocks.at[pl.ds(r * slots, slots)], held_ref.at[pl.ds(r * slots, slots)], sems.at[r])
        for r in range(1, own)
    ]
    for copy in copies:
        copy.start()

    def arrive(r):
        for copy in copies if r is None else copies[r - 1 : r] if r else []:
            copy.wait()

    score_entries(
        entries, 0, table_ref, costs, held_ref, tau_ref, elasticity_ref, weights_ref, top_ref, norm_ref, arrive
    )


def far_kernel(entries, first, table_ref, held_ref, tau_ref, elasticity_ref, cost_ref, weights_ref, top_ref, norm_ref):
    score_entries(entries, first, table_ref, [cost_ref], held_ref, tau_ref, elasticity_ref, weights_ref, top_ref, norm_ref)


def push_entries(entries, distances, table_ref, adjoint_of, held_ref, total_ref):
    own, capacity = entries.own, entries.capacity

    def pushed(entry):
        return lax.dot_general(
            adjoint_of(entry),
            held_ref[entries.slot(table_ref, entry)],
            CONTRACT_LAST,
            preferred_element_type=F32,
        )

    if entries.dense:
        for block, distance in enumerate(distances):
            for place in range(own):
                terms = [pushed(distance * capacity + r * own + place) for r in range(own)]
                total_ref[block * own + place] = sum(terms[1:], terms[0]).astype(total_ref.dtype)
        return
    total_ref[...] = jnp.zeros(total_ref.shape, total_ref.dtype)
    for block, distance in enumerate(distances):
        for entry in range(distance * capacity, (distance + 1) * capacity):
            total_ref[block * own + entries.place(table_ref, entry)] += pushed(entry)


def adjoint_kernel(entries, order, distances, *refs):
    n = len(order)
    table_ref, held_ref, cotangent_ref = refs[:3]
    weights, tops, norms = ([refs[3 + c * n + order.index(k)] for k in range(n)] for c in range(3))
    adjoint_ref, tau_grad_ref, logsum_ref, partial_ref, factor_ref, tau_rows_ref, total_ref = refs[3 + 3 * n :]
    own, capacity = entries.own, entries.capacity
    piece = weights[0].shape[0]
    tau_rows_ref[...] = jnp.zeros(tau_rows_ref.shape, F32)
    for r in range(own):
        top = functools.reduce(jnp.maximum, [ref[r] for ref in tops])
        shrink = [jnp.exp(ref[r] - top) for ref in tops]
        norm = sum(ref[r] * factor for ref, factor in zip(norms, shrink))
        logsum_ref[r] = top + jnp.log(norm)
        scale = cotangent_ref[r] / norm
        for k in range(n):
            factor_ref[k, r] = scale * shrink[k]
    for k in range(n):
        factor_ref[k, own] = jnp.zeros(factor_ref.shape[2:], F32)

    def adjoint(entry):
        k, i = divmod(entry, piece)
        value = factor_ref[k, entries.importer(table_ref, entry)] * weights[k][i]
        tau_rows_ref[pl.ds(entries.row(table_ref, entry), 1)] = jnp.sum(value, axis=0, keepdims=True)
        return value.astype(BF16)

    push_entries(entries, distances, table_ref, adjoint, held_ref, total_ref)
    partial_ref[...] = total_ref[...].astype(BF16)
    for entry in range(entries.count):
        if entry // capacity not in distances:
            adjoint_ref[entry] = adjoint(entry)
    tau_grad_ref[...] = tau_rows_ref[pl.ds(0, entries.slot_count)]


def push_kernel(entries, distances, table_ref, held_ref, adjoint_ref, partial_ref, total_ref):
    push_entries(entries, distances, table_ref, lambda entry: adjoint_ref[entry], held_ref, total_ref)
    partial_ref[...] = total_ref[...].astype(partial_ref.dtype)


def finish_kernel(n, *refs):
    own_sum_ref, received = refs[0], refs[1 : 1 + n]
    io_ref, share_ref, logsum_ref, elasticity_ref, tau_ref, tau_received_ref = refs[1 + n : 7 + n]
    prices_ref, price_grad_ref, wage_grad_ref, tau_grad_ref = refs[7 + n :]
    tau_grad_ref[...] = tau_ref[...] + tau_received_ref[...]
    for r in range(own_sum_ref.shape[0]):
        prices_ref[r] = (-logsum_ref[r] / elasticity_ref[...]).astype(BF16)
        cost_adjoint = own_sum_ref[r]
        for ref in received:
            cost_adjoint = cost_adjoint + ref[r].astype(F32)
        price_grad_ref[r] = lax.dot_general(
            cost_adjoint.astype(BF16), io_ref[r], CONTRACT_LAST, preferred_element_type=F32
        )
        wage_grad_ref[r] = jnp.sum(cost_adjoint * share_ref[pl.ds(r, 1)], axis=1)


def shards(
    log_prices,
    log_wages,
    labor_share,
    io_coeffs,
    pair_blocks,
    log_tau,
    elasticity,
    partners,
    list_lengths,
    price_cotangent,
):
    own, episodes, sectors = log_prices.shape
    slots = pair_blocks.shape[1]
    reg_count = lax.axis_size("reg")
    ep_count = lax.axis_size("ep")
    entries = Entries(own, slots, reg_count)
    blocks = pair_blocks.reshape(own * slots, sectors, sectors)
    row = (episodes, sectors)
    stages = radices(reg_count)
    last_radix = stages[-1]
    last_stride = reg_count // last_radix
    capacity = entries.capacity

    unit_cost = (
        labor_share[:, None, :] * log_wages[:, :, None]
        + jnp.einsum("iek,ikj->iej", log_prices, io_coeffs, preferred_element_type=F32)
    ).astype(BF16)

    held, tau, cotangent, elastic, cost_copy, table = pl.pallas_call(
        functools.partial(load_kernel, entries),
        out_shape=(
            shape(blocks.shape, BF16),
            shape((own * slots, sectors), F32),
            shape(price_cotangent.shape, F32),
            shape((1, sectors), F32),
            shape(unit_cost.shape, BF16),
            pltpu.SMEM((entries.columns * entries.stride,), jnp.int32),
        ),
        in_specs=[SMEM, VMEM] + [HBM] * 6,
        out_specs=(VMEM,) * 5 + (SMEM,),
        scratch_shapes=[
            pltpu.SMEM(partners.shape, jnp.int32),
            pltpu.SMEM(list_lengths.shape, jnp.int32),
            pltpu.SMEM((reg_count,), jnp.int32),
            pltpu.SemaphoreType.DMA((6,)),
        ],
        compiler_params=params(1),
        cost_estimate=effort(blocks.size),
        name="load",
    )(
        lax.axis_index("reg").reshape(1),
        unit_cost,
        in_hbm(blocks),
        in_hbm(log_tau.reshape(own * slots, sectors)),
        in_hbm(price_cotangent),
        in_hbm(elasticity.reshape(1, sectors)),
        in_hbm(partners),
        in_hbm(list_lengths),
    )

    near = [unit_cost]
    stride = 1
    for radix in stages[:-1]:
        if stride > 1:
            near[0] = cost_copy
        whole = jnp.concatenate(near, axis=0)
        near += [from_peer(whole, j * stride, "reg", reg_count) for j in range(1, radix)]
        stride *= radix
    near[0] = cost_copy
    whole = jnp.concatenate(near, axis=0)
    far = [from_peer(whole, j * stride, "reg", reg_count) for j in range(1, last_radix)]

    def scored(count):
        return (
            shape((count,) + row, F32),
            shape((own + 1,) + row, F32),
            shape((own + 1,) + row, F32),
        )

    piece = last_stride * capacity
    held, *near_scores = pl.pallas_call(
        functools.partial(near_kernel, entries, len(near)),
        out_shape=(shape(blocks.shape, BF16),) + scored(piece),
        in_specs=[SMEM, HBM] + [VMEM] * (3 + len(near)),
        out_specs=(VMEM,) * 4,
        scratch_shapes=[pltpu.SemaphoreType.DMA((own,))],
        input_output_aliases={2: 0},
        compiler_params=params(2),
        cost_estimate=effort(blocks.size),
        name="near",
    )(table, in_hbm(blocks), held, tau, elastic, *near)
    scores = [near_scores]
    for j, cost in enumerate(far, 1):
        scores.append(
            pl.pallas_call(
                functools.partial(far_kernel, entries, j * last_stride),
                out_shape=scored(piece),
                in_specs=[SMEM] + [VMEM] * 4,
                out_specs=(VMEM,) * 3,
                compiler_params=params(2),
                cost_estimate=effort(blocks.size // last_radix * 2),
                name="far",
            )(table, held, tau, elastic, cost)
        )
    order = [0, *range(2, last_radix), 1]
    radix = stages[0]
    groups = [range(j, reg_count, radix) for j in range(radix)]
    partial_dims = (reg_count // radix * own,) + row
    adjoint, tau_grad, logsum, partial = pl.pallas_call(
        functools.partial(adjoint_kernel, entries, order, groups[-1]),
        out_shape=(
            shape((entries.count,) + row, BF16),
            shape((own * slots, sectors), F32),
            shape((own,) + row, F32),
            shape(partial_dims, BF16),
        ),
        in_specs=[SMEM] + [VMEM] * (2 + 3 * last_radix),
        out_specs=(VMEM,) * 4,
        scratch_shapes=[
            pltpu.VMEM((last_radix, own + 1) + row, F32),
            pltpu.VMEM((own * slots + 8, sectors), F32),
            pltpu.VMEM(partial_dims, F32),
        ],
        compiler_params=params(8),
        cost_estimate=effort(blocks.size),
        name="adjoint",
    )(table, held, cotangent, *[scores[k][c] for c in range(3) for k in order])

    def push(j, dtype):
        return pl.pallas_call(
            functools.partial(push_kernel, entries, groups[j]),
            out_shape=shape(partial_dims, dtype),
            in_specs=[SMEM, VMEM, VMEM],
            out_specs=VMEM,
            scratch_shapes=[pltpu.VMEM(partial_dims, F32)],
            compiler_params=params(8),
            cost_estimate=effort(blocks.size),
            name="push",
        )(table, held, adjoint)

    received = [to_peer(partial, radix - 1, "reg", reg_count)] if radix > 1 else []
    for j in range(radix - 2, 0, -1):
        received.append(to_peer(push(j, BF16), j, "reg", reg_count))
    summed = push(0, F32) if radix > 1 else partial.astype(F32)
    stride = 1
    for following in stages[1:]:
        for block in received:
            summed = summed + block.astype(F32)
        stride *= radix
        radix = following
        parts = summed.reshape((-1, radix, own) + row)
        received = [
            to_peer(parts[:, j].reshape((-1,) + row).astype(BF16), j * stride, "reg", reg_count)
            for j in range(radix - 1, 0, -1)
        ]
        summed = parts[:, 0].reshape((-1,) + row)

    if is_power_of_two(ep_count):
        tau_received = jnp.zeros_like(tau_grad)
        distance = 1
        while distance < ep_count:
            tau_grad = tau_grad + tau_received if distance > 1 else tau_grad
            tau_received = to_peer(tau_grad, distance, "ep", ep_count)
            distance *= 2
    else:
        tau_grad = lax.psum(tau_grad, "ep")
        tau_received = jnp.zeros_like(tau_grad)

    new_prices, price_grad, wage_grad, tau_grad = pl.pallas_call(
        functools.partial(finish_kernel, len(received)),
        out_shape=(
            shape((own,) + row, BF16),
            shape((own,) + row, F32),
            shape((own, episodes), F32),
            shape(tau_grad.shape, F32),
        ),
        in_specs=[VMEM] * (7 + len(received)),
        out_specs=(VMEM,) * 4,
        compiler_params=params(4),
        name="finish",
    )(summed, *received, io_coeffs, labor_share, logsum, elastic, tau_grad, tau_received)
    return new_prices, price_grad, wage_grad, tau_grad.reshape(own, slots, sectors)


def solution(mesh):
    return jax.shard_map(
        shards,
        mesh=mesh,
        in_specs=(
            P("reg", "ep", None),
            P("reg", "ep"),
            P("reg", None),
            P("reg", None, None),
            P("reg", None, None, None),
            P("reg", None, None),
            P(),
            P(),
            P(),
            P("reg", "ep", None),
        ),
        out_specs=(
            P("reg", "ep", None),
            P("reg", "ep", None),
            P("reg", "ep"),
            P("reg", None, None),
        ),
        check_vma=False,
    )
```

```python
import functools

import jax
import jax.numpy as jnp
from jax import lax
from jax.experimental import pallas as pl
from jax.experimental.pallas import tpu as pltpu
from jax.sharding import PartitionSpec as P

F32 = jnp.float32
BF16 = jnp.bfloat16
CONTRACT_LAST = (((1,), (1,)), ((), ()))
LOWEST = -1e30
VMEM = pl.BlockSpec(memory_space=pltpu.VMEM)
SMEM = pl.BlockSpec(memory_space=pltpu.SMEM)
HBM = pl.BlockSpec(memory_space=pltpu.HBM)


def is_power_of_two(n):
    return n & (n - 1) == 0


def peer(i, distance, n):
    return i ^ distance if is_power_of_two(n) else (i + distance) % n


def distance_of(owner, me, n):
    return owner ^ me if is_power_of_two(n) else lax.rem(owner - me + n, n)


def radices(n):
    stages = []
    if n.bit_length() % 2 == 0 and is_power_of_two(n):
        stages.append(2)
        n //= 2
    while n % 4 == 0:
        stages.append(4)
        n //= 4
    if n > 1 or not stages:
        stages.append(n)
    return stages


def from_peer(x, distance, axis, n):
    return lax.ppermute(x, axis, [(peer(i, distance, n), i) for i in range(n)])


def to_peer(x, distance, axis, n):
    return lax.ppermute(x, axis, [(i, peer(i, distance, n)) for i in range(n)])


def shape(dims, dtype):
    return jax.ShapeDtypeStruct(dims, dtype)


def params(mebibytes):
    return pltpu.CompilerParams(vmem_limit_bytes=mebibytes << 20)


def effort(size):
    return pl.CostEstimate(flops=0, bytes_accessed=size, transcendentals=0)


def in_hbm(x):
    return pltpu.with_memory_space_constraint(x, pltpu.HBM)


class Entries:
    def __init__(self, own, slots, reg_count):
        self.own, self.slots, self.reg_count = own, slots, reg_count
        self.slot_count = own * slots
        self.loaded_first = 3 * own * slots // 8
        self.dense = reg_count * own <= slots
        self.capacity = own * own if self.dense else -(-own * slots // reg_count)
        self.count = self.capacity * reg_count
        self.stride = self.count + 1
        self.columns = 2 if self.dense else 4

    def numbers(self, distances):
        return [distance * self.capacity + i for distance in distances for i in range(self.capacity)]

    def turned(self, distances):
        if not self.dense:
            return []
        return self.numbers(distances)

    def slot(self, table, entry):
        return table[entry]

    def row(self, table, entry):
        return table[self.stride + entry]

    def live(self, table, entry):
        return self.row(table, entry) < self.slot_count

    def importer(self, table, entry):
        return entry % self.capacity // self.own if self.dense else table[2 * self.stride + entry]

    def place(self, table, entry):
        return entry % self.own if self.dense else table[3 * self.stride + entry]

    def fill(self, table, found, partners, lengths, me):
        own = self.own
        for entry in range(self.stride):
            for column, value in enumerate((0, self.slot_count, own, 0)[: self.columns]):
                table[column * self.stride + entry] = value
        if not self.dense:
            for distance in range(self.reg_count):
                found[distance] = 0
        for r in range(own):
            length = lengths[me * own + r]
            for s in range(self.slots):
                partner = partners[me * own + r, s]
                distance = distance_of(lax.div(partner, own), me, self.reg_count)
                place = lax.rem(partner, own)
                slot = r * self.slots + s
                if self.dense:
                    entry = distance * self.capacity + r * own + place
                    columns = (slot, slot)
                else:
                    entry = distance * self.capacity + found[distance]
                    columns = (slot, slot, r, place)
                    found[distance] += (s < length).astype(jnp.int32)
                entry = jnp.minimum(jnp.where(s < length, entry, self.count), self.count)
                for column, value in enumerate(columns):
                    table[column * self.stride + entry] = value


def load_kernel(
    entries, me_ref, cost_ref, blocks, tau, cotangent, elasticity, partners, lengths,
    held_ref, tau_ref, cotangent_ref, elasticity_ref, cost_copy_ref, table_ref,
    partners_ref, lengths_ref, found_ref, sems,
):
    copies = [
        pltpu.make_async_copy(source, target, sems.at[i])
        for i, (source, target) in enumerate(
            (
                (partners, partners_ref),
                (lengths, lengths_ref),
                (tau, tau_ref),
                (cotangent, cotangent_ref),
                (elasticity, elasticity_ref),
                (blocks.at[pl.ds(0, entries.loaded_first)], held_ref.at[pl.ds(0, entries.loaded_first)]),
            )
        )
    ]
    for copy in copies:
        copy.start()
    cost_copy_ref[...] = cost_ref[...]
    copies[0].wait()
    copies[1].wait()
    entries.fill(table_ref, found_ref, partners_ref, lengths_ref, me_ref[0])
    for copy in copies[2:]:
        copy.wait()


def score_entries(
    entries, distances, table_ref, costs, held_ref, tau_ref, elasticity_ref, weights_ref, top_ref, norm_ref,
    arrive=lambda r: None,
):
    own, capacity = entries.own, entries.capacity
    numbers = entries.numbers(distances)
    count = len(numbers)
    scale = -elasticity_ref[...]
    lowest = jnp.full(top_ref.shape[1:], LOWEST, F32)
    zero = jnp.zeros(top_ref.shape[1:], F32)
    rows = [(ref, block) for ref in costs for block in range(ref.shape[0] // own)]

    def score(i):
        entry = numbers[i]
        ref, block = rows[i // capacity]
        slot = entries.slot(table_ref, entry)
        cost = ref[block * own + entries.place(table_ref, entry)]
        landed = jnp.dot(cost, held_ref[slot], preferred_element_type=F32) + tau_ref[pl.ds(slot, 1)]
        return scale * landed

    if entries.dense:
        for r in range(own):
            arrive(r)
            members = [i for i in range(count) if entries.importer(table_ref, numbers[i]) == r]
            scores = [jnp.where(entries.live(table_ref, numbers[i]), score(i), -jnp.inf) for i in members]
            top = functools.reduce(jnp.maximum, scores, lowest)
            norm = zero
            for i, value in zip(members, scores):
                weight = jnp.exp(value - top)
                weights_ref[i] = weight
                norm = norm + weight
            top_ref[r] = top
            norm_ref[r] = norm
        return
    arrive(None)
    top_ref[...] = jnp.full(top_ref.shape, LOWEST, F32)
    norm_ref[...] = jnp.zeros(norm_ref.shape, F32)
    for i in range(count):
        importer = entries.importer(table_ref, numbers[i])
        value = score(i)
        weights_ref[i] = value
        top_ref[importer] = jnp.maximum(top_ref[importer], value)
    for i in range(count):
        importer = entries.importer(table_ref, numbers[i])
        weight = jnp.exp(weights_ref[i] - top_ref[importer])
        weights_ref[i] = weight
        norm_ref[importer] += weight


def near_kernel(entries, distances, turned, n_costs, *refs):
    table_ref, blocks, _, tau_ref, elasticity_ref = refs[:5]
    costs = refs[5 : 5 + n_costs]
    held_ref, weights_ref, top_ref, norm_ref, turned_ref, sems = refs[5 + n_costs :]
    copies = []
    for r in range(entries.own):
        start, stop = max(r * entries.slots, entries.loaded_first), (r + 1) * entries.slots
        if start < stop:
            part = pl.ds(start, stop - start)
            copies.append(pltpu.make_async_copy(blocks.at[part], held_ref.at[part], sems.at[r]))
    for copy in copies:
        copy.start()
    skipped = entries.own - len(copies)

    def arrive(r):
        for copy in copies if r is None else copies[r - skipped : r - skipped + 1] if r >= skipped else []:
            copy.wait()
        for i, entry in enumerate(turned):
            if r is None or entries.importer(table_ref, entry) == r:
                turned_ref[i] = held_ref[entries.slot(table_ref, entry)].T

    score_entries(
        entries, distances, table_ref, costs, held_ref, tau_ref, elasticity_ref, weights_ref, top_ref, norm_ref, arrive
    )


def far_kernel(entries, distances, table_ref, held_ref, tau_ref, elasticity_ref, cost_ref, weights_ref, top_ref, norm_ref):
    score_entries(
        entries, distances, table_ref, [cost_ref], held_ref, tau_ref, elasticity_ref, weights_ref, top_ref, norm_ref
    )


def push_entries(entries, distances, table_ref, adjoint_of, held_ref, total_ref, turned=(), turned_ref=None):
    own, capacity = entries.own, entries.capacity

    def pushed(entry):
        if entry in turned:
            return jnp.dot(adjoint_of(entry), turned_ref[turned.index(entry)], preferred_element_type=F32)
        return lax.dot_general(
            adjoint_of(entry),
            held_ref[entries.slot(table_ref, entry)],
            CONTRACT_LAST,
            preferred_element_type=F32,
        )

    if entries.dense:
        for block, distance in enumerate(distances):
            for place in range(own):
                terms = [pushed(distance * capacity + r * own + place) for r in range(own)]
                total_ref[block * own + place] = sum(terms[1:], terms[0]).astype(total_ref.dtype)
        return
    total_ref[...] = jnp.zeros(total_ref.shape, total_ref.dtype)
    for block, distance in enumerate(distances):
        for entry in range(distance * capacity, (distance + 1) * capacity):
            total_ref[block * own + entries.place(table_ref, entry)] += pushed(entry)


def adjoint_kernel(entries, pieces, distances, turned, *refs):
    n = len(pieces)
    piece_of = {entry: (k, i) for k, piece in enumerate(pieces) for i, entry in enumerate(entries.numbers(piece))}
    table_ref, held_ref, turned_ref, cotangent_ref = refs[:4]
    weights, tops, norms = refs[4 : 4 + n], refs[4 + n : 4 + 2 * n], refs[4 + 2 * n : 4 + 3 * n]
    adjoint_ref, tau_grad_ref, logsum_ref, partial_ref, factor_ref, tau_rows_ref, total_ref = refs[4 + 3 * n :]
    own, capacity = entries.own, entries.capacity
    tau_rows_ref[...] = jnp.zeros(tau_rows_ref.shape, F32)
    for r in range(own):
        top = functools.reduce(jnp.maximum, [ref[r] for ref in tops])
        shrink = [jnp.exp(ref[r] - top) for ref in tops]
        norm = sum(ref[r] * factor for ref, factor in zip(norms, shrink))
        logsum_ref[r] = top + jnp.log(norm)
        scale = cotangent_ref[r] / norm
        for k in range(n):
            factor_ref[k, r] = scale * shrink[k]
    for k in range(n):
        factor_ref[k, own] = jnp.zeros(factor_ref.shape[2:], F32)

    def adjoint(entry):
        k, i = piece_of[entry]
        value = factor_ref[k, entries.importer(table_ref, entry)] * weights[k][i]
        tau_rows_ref[pl.ds(entries.row(table_ref, entry), 1)] = jnp.sum(value, axis=0, keepdims=True)
        return value.astype(BF16)

    push_entries(entries, distances, table_ref, adjoint, held_ref, total_ref, turned, turned_ref)
    partial_ref[...] = total_ref[...].astype(BF16)
    for entry in range(entries.count):
        if entry // capacity not in distances:
            adjoint_ref[entry] = adjoint(entry)
    tau_grad_ref[...] = tau_rows_ref[pl.ds(0, entries.slot_count)]


def push_kernel(entries, distances, table_ref, held_ref, adjoint_ref, partial_ref, total_ref):
    push_entries(entries, distances, table_ref, lambda entry: adjoint_ref[entry], held_ref, total_ref)
    partial_ref[...] = total_ref[...].astype(partial_ref.dtype)


def finish_kernel(n, *refs):
    own_sum_ref, received = refs[0], refs[1 : 1 + n]
    io_ref, share_ref, logsum_ref, elasticity_ref, tau_ref, tau_received_ref = refs[1 + n : 7 + n]
    prices_ref, price_grad_ref, wage_grad_ref, tau_grad_ref = refs[7 + n :]
    tau_grad_ref[...] = tau_ref[...] + tau_received_ref[...]
    for r in range(own_sum_ref.shape[0]):
        prices_ref[r] = (-logsum_ref[r] / elasticity_ref[...]).astype(BF16)
        cost_adjoint = own_sum_ref[r]
        for ref in received:
            cost_adjoint = cost_adjoint + ref[r].astype(F32)
        price_grad_ref[r] = lax.dot_general(
            cost_adjoint.astype(BF16), io_ref[r], CONTRACT_LAST, preferred_element_type=F32
        )
        wage_grad_ref[r] = jnp.sum(cost_adjoint * share_ref[pl.ds(r, 1)], axis=1)


def shards(
    log_prices,
    log_wages,
    labor_share,
    io_coeffs,
    pair_blocks,
    log_tau,
    elasticity,
    partners,
    list_lengths,
    price_cotangent,
):
    own, episodes, sectors = log_prices.shape
    slots = pair_blocks.shape[1]
    reg_count = lax.axis_size("reg")
    ep_count = lax.axis_size("ep")
    entries = Entries(own, slots, reg_count)
    blocks = pair_blocks.reshape(own * slots, sectors, sectors)
    row = (episodes, sectors)
    stages = radices(reg_count)

    unit_cost = (
        labor_share[:, None, :] * log_wages[:, :, None]
        + jnp.einsum("iek,ikj->iej", log_prices, io_coeffs, preferred_element_type=F32)
    ).astype(BF16)

    held, tau, cotangent, elastic, cost_copy, table = pl.pallas_call(
        functools.partial(load_kernel, entries),
        out_shape=(
            shape(blocks.shape, BF16),
            shape((own * slots, sectors), F32),
            shape(price_cotangent.shape, F32),
            shape((1, sectors), F32),
            shape(unit_cost.shape, BF16),
            pltpu.SMEM((entries.columns * entries.stride,), jnp.int32),
        ),
        in_specs=[SMEM, VMEM] + [HBM] * 6,
        out_specs=(VMEM,) * 5 + (SMEM,),
        scratch_shapes=[
            pltpu.SMEM(partners.shape, jnp.int32),
            pltpu.SMEM(list_lengths.shape, jnp.int32),
            pltpu.SMEM((reg_count,), jnp.int32),
            pltpu.SemaphoreType.DMA((6,)),
        ],
        compiler_params=params(1),
        cost_estimate=effort(blocks.size),
        name="load",
    )(
        lax.axis_index("reg").reshape(1),
        unit_cost,
        in_hbm(blocks),
        in_hbm(log_tau.reshape(own * slots, sectors)),
        in_hbm(price_cotangent),
        in_hbm(elasticity.reshape(1, sectors)),
        in_hbm(partners),
        in_hbm(list_lengths),
    )

    near, near_distances = [unit_cost], [0]
    stride = reg_count
    for radix in reversed(stages):
        stride //= radix
        whole, distances = jnp.concatenate(near, axis=0), near_distances
        order = [*range(2, radix), 1]
        received = [from_peer(whole, j * stride, "reg", reg_count) for j in order]
        reached = [[d + j * stride for d in distances] for j in order]
        near[0] = cost_copy
        if stride > 1:
            near = near + received
            near_distances = sum(reached, distances)
    pieces = [near_distances] + reached

    def scored(distances):
        return (
            shape((len(distances) * entries.capacity,) + row, F32),
            shape((own + 1,) + row, F32),
            shape((own + 1,) + row, F32),
        )

    radix = stages[0]
    groups = [range(j, reg_count, radix) for j in range(radix)]
    turned = entries.turned(groups[-1])
    held, *near_scores, turned_blocks = pl.pallas_call(
        functools.partial(near_kernel, entries, near_distances, turned, len(near)),
        out_shape=(shape(blocks.shape, BF16),)
        + scored(near_distances)
        + (shape((max(len(turned), 1), sectors, sectors), BF16),),
        in_specs=[SMEM, HBM] + [VMEM] * (3 + len(near)),
        out_specs=(VMEM,) * 5,
        scratch_shapes=[pltpu.SemaphoreType.DMA((own,))],
        input_output_aliases={2: 0},
        compiler_params=params(2),
        cost_estimate=effort(blocks.size),
        name="near",
    )(table, in_hbm(blocks), held, tau, elastic, *near)
    scores = [near_scores]
    for cost, distances in zip(received, reached):
        scores.append(
            pl.pallas_call(
                functools.partial(far_kernel, entries, distances),
                out_shape=scored(distances),
                in_specs=[SMEM] + [VMEM] * 4,
                out_specs=(VMEM,) * 3,
                compiler_params=params(2),
                cost_estimate=effort(blocks.size // len(pieces) * 2),
                name="far",
            )(table, held, tau, elastic, cost)
        )
    partial_dims = (reg_count // radix * own,) + row
    adjoint, tau_grad, logsum, partial = pl.pallas_call(
        functools.partial(adjoint_kernel, entries, pieces, groups[-1], turned),
        out_shape=(
            shape((entries.count,) + row, BF16),
            shape((own * slots, sectors), F32),
            shape((own,) + row, F32),
            shape(partial_dims, BF16),
        ),
        in_specs=[SMEM] + [VMEM] * (3 + 3 * len(pieces)),
        out_specs=(VMEM,) * 4,
        scratch_shapes=[
            pltpu.VMEM((len(pieces), own + 1) + row, F32),
            pltpu.VMEM((own * slots + 8, sectors), F32),
            pltpu.VMEM(partial_dims, F32),
        ],
        compiler_params=params(8),
        cost_estimate=effort(blocks.size),
        name="adjoint",
    )(table, held, turned_blocks, cotangent, *[score[c] for c in range(3) for score in scores])

    def push(j, dtype):
        return pl.pallas_call(
            functools.partial(push_kernel, entries, groups[j]),
            out_shape=shape(partial_dims, dtype),
            in_specs=[SMEM, VMEM, VMEM],
            out_specs=VMEM,
            scratch_shapes=[pltpu.VMEM(partial_dims, F32)],
            compiler_params=params(8),
            cost_estimate=effort(blocks.size),
            name="push",
        )(table, held, adjoint)

    received = [to_peer(partial, radix - 1, "reg", reg_count)] if radix > 1 else []
    for j in range(radix - 2, 0, -1):
        received.append(to_peer(push(j, BF16), j, "reg", reg_count))
    summed = push(0, F32) if radix > 1 else partial.astype(F32)
    stride = 1
    for following in stages[1:]:
        for block in received:
            summed = summed + block.astype(F32)
        stride *= radix
        radix = following
        parts = summed.reshape((-1, radix, own) + row)
        received = [
            to_peer(parts[:, j].reshape((-1,) + row).astype(BF16), j * stride, "reg", reg_count)
            for j in range(radix - 1, 0, -1)
        ]
        summed = parts[:, 0].reshape((-1,) + row)

    if is_power_of_two(ep_count):
        tau_received = jnp.zeros_like(tau_grad)
        distance = 1
        while distance < ep_count:
            tau_grad = tau_grad + tau_received if distance > 1 else tau_grad
            tau_received = to_peer(tau_grad, distance, "ep", ep_count)
            distance *= 2
    else:
        tau_grad = lax.psum(tau_grad, "ep")
        tau_received = jnp.zeros_like(tau_grad)

    new_prices, price_grad, wage_grad, tau_grad = pl.pallas_call(
        functools.partial(finish_kernel, len(received)),
        out_shape=(
            shape((own,) + row, BF16),
            shape((own,) + row, F32),
            shape((own, episodes), F32),
            shape(tau_grad.shape, F32),
        ),
        in_specs=[VMEM] * (7 + len(received)),
        out_specs=(VMEM,) * 4,
        compiler_params=params(4),
        name="finish",
    )(summed, *received, io_coeffs, labor_share, logsum, elastic, tau_grad, tau_received)
    return new_prices, price_grad, wage_grad, tau_grad.reshape(own, slots, sectors)


def solution(mesh):
    return jax.shard_map(
        shards,
        mesh=mesh,
        in_specs=(
            P("reg", "ep", None),
            P("reg", "ep"),
            P("reg", None),
            P("reg", None, None),
            P("reg", None, None, None),
            P("reg", None, None),
            P(),
            P(),
            P(),
            P("reg", "ep", None),
        ),
        out_specs=(
            P("reg", "ep", None),
            P("reg", "ep", None),
            P("reg", "ep"),
            P("reg", None, None),
        ),
        check_vma=False,
    )
```

```python
import functools

import jax
import jax.numpy as jnp
from jax import lax
from jax.experimental import pallas as pl
from jax.experimental.pallas import tpu as pltpu
from jax.sharding import PartitionSpec as P

F32 = jnp.float32
BF16 = jnp.bfloat16
CONTRACT_LAST = (((1,), (1,)), ((), ()))
LOWEST = -1e30
VMEM = pl.BlockSpec(memory_space=pltpu.VMEM)
SMEM = pl.BlockSpec(memory_space=pltpu.SMEM)
HBM = pl.BlockSpec(memory_space=pltpu.HBM)


def is_power_of_two(n):
    return n & (n - 1) == 0


def peer(i, distance, n):
    return i ^ distance if is_power_of_two(n) else (i + distance) % n


def distance_of(owner, me, n):
    return owner ^ me if is_power_of_two(n) else lax.rem(owner - me + n, n)


def radices(n):
    stages = []
    if n.bit_length() % 2 == 0 and is_power_of_two(n):
        stages.append(2)
        n //= 2
    while n % 4 == 0:
        stages.append(4)
        n //= 4
    if n > 1 or not stages:
        stages.append(n)
    return stages


def from_peer(x, distance, axis, n):
    return lax.ppermute(x, axis, [(peer(i, distance, n), i) for i in range(n)])


def to_peer(x, distance, axis, n):
    return lax.ppermute(x, axis, [(i, peer(i, distance, n)) for i in range(n)])


def shape(dims, dtype):
    return jax.ShapeDtypeStruct(dims, dtype)


def params(mebibytes):
    return pltpu.CompilerParams(vmem_limit_bytes=mebibytes << 20)


def effort(size):
    return pl.CostEstimate(flops=0, bytes_accessed=size, transcendentals=0)


def in_hbm(x):
    return pltpu.with_memory_space_constraint(x, pltpu.HBM)


class Entries:
    def __init__(self, own, slots, reg_count):
        self.own, self.slots, self.reg_count = own, slots, reg_count
        self.slot_count = own * slots
        self.loaded_first = 4 * own * slots // 8
        self.dense = reg_count * own <= slots
        self.capacity = own * own if self.dense else -(-own * slots // reg_count)
        self.count = self.capacity * reg_count
        self.stride = self.count + 1
        self.columns = 2 if self.dense else 4

    def numbers(self, distances):
        return [distance * self.capacity + i for distance in distances for i in range(self.capacity)]

    def turned(self, distances):
        if not self.dense:
            return []
        return self.numbers(distances)

    def slot(self, table, entry):
        return table[entry]

    def row(self, table, entry):
        return table[self.stride + entry]

    def live(self, table, entry):
        return self.row(table, entry) < self.slot_count

    def importer(self, table, entry):
        return entry % self.capacity // self.own if self.dense else table[2 * self.stride + entry]

    def place(self, table, entry):
        return entry % self.own if self.dense else table[3 * self.stride + entry]

    def fill(self, table, found, partners, lengths, me):
        own = self.own
        for entry in range(self.stride):
            for column, value in enumerate((0, self.slot_count, own, 0)[: self.columns]):
                table[column * self.stride + entry] = value
        if not self.dense:
            for distance in range(self.reg_count):
                found[distance] = 0
        for r in range(own):
            length = lengths[me * own + r]
            for s in range(self.slots):
                partner = partners[me * own + r, s]
                distance = distance_of(lax.div(partner, own), me, self.reg_count)
                place = lax.rem(partner, own)
                slot = r * self.slots + s
                if self.dense:
                    entry = distance * self.capacity + r * own + place
                    columns = (slot, slot)
                else:
                    entry = distance * self.capacity + found[distance]
                    columns = (slot, slot, r, place)
                    found[distance] += (s < length).astype(jnp.int32)
                entry = jnp.minimum(jnp.where(s < length, entry, self.count), self.count)
                for column, value in enumerate(columns):
                    table[column * self.stride + entry] = value


def load_kernel(
    entries, me_ref, cost_ref, blocks, tau, cotangent, elasticity, partners, lengths,
    held_ref, tau_ref, cotangent_ref, elasticity_ref, cost_copy_ref, table_ref,
    partners_ref, lengths_ref, found_ref, sems,
):
    copies = [
        pltpu.make_async_copy(source, target, sems.at[i])
        for i, (source, target) in enumerate(
            (
                (partners, partners_ref),
                (lengths, lengths_ref),
                (tau, tau_ref),
                (cotangent, cotangent_ref),
                (elasticity, elasticity_ref),
                (blocks.at[pl.ds(0, entries.loaded_first)], held_ref.at[pl.ds(0, entries.loaded_first)]),
            )
        )
    ]
    for copy in copies:
        copy.start()
    cost_copy_ref[...] = cost_ref[...]
    copies[0].wait()
    copies[1].wait()
    entries.fill(table_ref, found_ref, partners_ref, lengths_ref, me_ref[0])
    for copy in copies[2:]:
        copy.wait()


def scorer(entries, numbers, table_ref, costs, held_ref, tau_ref, elasticity_ref):
    scale = -elasticity_ref[...]
    rows = [(ref, block) for ref in costs for block in range(ref.shape[0] // entries.own)]

    def score(i):
        entry = numbers[i]
        ref, block = rows[i // entries.capacity]
        slot = entries.slot(table_ref, entry)
        cost = ref[block * entries.own + entries.place(table_ref, entry)]
        landed = jnp.dot(cost, held_ref[slot], preferred_element_type=F32) + tau_ref[pl.ds(slot, 1)]
        value = scale * landed
        return jnp.where(entries.live(table_ref, entry), value, -jnp.inf) if entries.dense else value

    return score


def score_entries(
    entries, distances, table_ref, costs, held_ref, tau_ref, elasticity_ref, weights_ref, top_ref, norm_ref,
    arrive=lambda r: None,
):
    own = entries.own
    numbers = entries.numbers(distances)
    count = len(numbers)
    lowest = jnp.full(top_ref.shape[1:], LOWEST, F32)
    zero = jnp.zeros(top_ref.shape[1:], F32)
    score = scorer(entries, numbers, table_ref, costs, held_ref, tau_ref, elasticity_ref)
    if entries.dense:
        for r in range(own):
            arrive(r)
            members = [i for i in range(count) if entries.importer(table_ref, numbers[i]) == r]
            scores = [score(i) for i in members]
            top = functools.reduce(jnp.maximum, scores, lowest)
            norm = zero
            for i, value in zip(members, scores):
                weight = jnp.exp(value - top)
                weights_ref[i] = weight
                norm = norm + weight
            top_ref[r] = top
            norm_ref[r] = norm
        return
    arrive(None)
    top_ref[...] = jnp.full(top_ref.shape, LOWEST, F32)
    norm_ref[...] = jnp.zeros(norm_ref.shape, F32)
    for i in range(count):
        importer = entries.importer(table_ref, numbers[i])
        value = score(i)
        weights_ref[i] = value
        top_ref[importer] = jnp.maximum(top_ref[importer], value)
    for i in range(count):
        importer = entries.importer(table_ref, numbers[i])
        weight = jnp.exp(weights_ref[i] - top_ref[importer])
        weights_ref[i] = weight
        norm_ref[importer] += weight


def near_kernel(entries, distances, turned, n_costs, *refs):
    table_ref, blocks, _, tau_ref, elasticity_ref = refs[:5]
    costs = refs[5 : 5 + n_costs]
    held_ref, weights_ref, top_ref, norm_ref, turned_ref, sems = refs[5 + n_costs :]
    copies = []
    for r in range(entries.own):
        start, stop = max(r * entries.slots, entries.loaded_first), (r + 1) * entries.slots
        if start < stop:
            part = pl.ds(start, stop - start)
            copies.append(pltpu.make_async_copy(blocks.at[part], held_ref.at[part], sems.at[r]))
    for copy in copies:
        copy.start()
    skipped = entries.own - len(copies)

    def arrive(r):
        for copy in copies if r is None else copies[r - skipped : r - skipped + 1] if r >= skipped else []:
            copy.wait()
        for i, entry in enumerate(turned):
            if r is None or entries.importer(table_ref, entry) == r:
                turned_ref[i] = held_ref[entries.slot(table_ref, entry)].T

    score_entries(
        entries, distances, table_ref, costs, held_ref, tau_ref, elasticity_ref, weights_ref, top_ref, norm_ref, arrive
    )


def push_entries(entries, distances, table_ref, adjoint_of, held_ref, total_ref):
    own, capacity = entries.own, entries.capacity

    def pushed(entry):
        return lax.dot_general(
            adjoint_of(entry),
            held_ref[entries.slot(table_ref, entry)],
            CONTRACT_LAST,
            preferred_element_type=F32,
        )

    if entries.dense:
        for block, distance in enumerate(distances):
            for place in range(own):
                terms = [pushed(distance * capacity + r * own + place) for r in range(own)]
                total_ref[block * own + place] = sum(terms[1:], terms[0]).astype(total_ref.dtype)
        return
    total_ref[...] = jnp.zeros(total_ref.shape, total_ref.dtype)
    for block, distance in enumerate(distances):
        for entry in range(distance * capacity, (distance + 1) * capacity):
            total_ref[block * own + entries.place(table_ref, entry)] += pushed(entry)


def adjoint_kernel(entries, near_distances, far_distances, group, turned, *refs):
    table_ref, held_ref, turned_ref, tau_ref, elasticity_ref, cotangent_ref, near_weights, near_top, near_norm = refs[:9]
    costs = refs[9:-10]
    adjoint_ref, tau_grad_ref, logsum_ref, partial_ref = refs[-10:-6]
    far_weights, far_top, far_norm, factor_ref, tau_rows_ref, total_ref = refs[-6:]
    own, capacity = entries.own, entries.capacity
    near, far = entries.numbers(near_distances), entries.numbers(far_distances)
    tau_rows_ref[...] = jnp.zeros(tau_rows_ref.shape, F32)

    def rounded(entry, value):
        tau_rows_ref[pl.ds(entries.row(table_ref, entry), 1)] = jnp.sum(value, axis=0, keepdims=True)
        return value.astype(BF16)

    def pushed(entry, value):
        if entry in turned:
            return jnp.dot(value, turned_ref[turned.index(entry)], preferred_element_type=F32)
        return lax.dot_general(
            value, held_ref[entries.slot(table_ref, entry)], CONTRACT_LAST, preferred_element_type=F32
        )

    if entries.dense:
        score = scorer(entries, far, table_ref, costs, held_ref, tau_ref, elasticity_ref)
        members = [[i for i, entry in enumerate(far) if entries.importer(None, entry) == r] for r in range(own)]

        def emit(r, entry, value):
            value = rounded(entry, value)
            if entry // capacity not in group:
                adjoint_ref[entry] = value
                return
            place = group.index(entry // capacity) * own + entries.place(None, entry)
            term = pushed(entry, value)
            total_ref[place] = term if r == 0 else total_ref[place] + term

        for r in range(own + 1):
            if r < own:
                for i in members[r]:
                    far_weights[i] = score(i)
            if r == 0:
                continue
            q = r - 1
            top = functools.reduce(jnp.maximum, [far_weights[i] for i in members[q]], near_top[q])
            weights = [jnp.exp(far_weights[i] - top) for i in members[q]]
            shrink = jnp.exp(near_top[q] - top)
            norm = sum(weights, near_norm[q] * shrink)
            logsum_ref[q] = top + jnp.log(norm)
            scale = cotangent_ref[q] / norm
            for i, weight in zip(members[q], weights):
                emit(q, far[i], scale * weight)
            scale = scale * shrink
            for i, entry in enumerate(near):
                if entries.importer(None, entry) == q:
                    emit(q, entry, scale * near_weights[i])
    else:
        score_entries(
            entries, far_distances, table_ref, costs, held_ref, tau_ref, elasticity_ref, far_weights, far_top, far_norm
        )
        for r in range(own):
            top = jnp.maximum(near_top[r], far_top[r])
            shrink = [jnp.exp(near_top[r] - top), jnp.exp(far_top[r] - top)]
            norm = near_norm[r] * shrink[0] + far_norm[r] * shrink[1]
            logsum_ref[r] = top + jnp.log(norm)
            for k in range(2):
                factor_ref[k, r] = cotangent_ref[r] / norm * shrink[k]
        for k in range(2):
            factor_ref[k, own] = jnp.zeros(factor_ref.shape[2:], F32)
        total_ref[...] = jnp.zeros(total_ref.shape, F32)
        for k, (numbers, weights_ref) in enumerate(((near, near_weights), (far, far_weights))):
            for i, entry in enumerate(numbers):
                value = rounded(entry, factor_ref[k, entries.importer(table_ref, entry)] * weights_ref[i])
                if entry // capacity in group:
                    place = group.index(entry // capacity) * own + entries.place(table_ref, entry)
                    total_ref[place] += pushed(entry, value)
                else:
                    adjoint_ref[entry] = value
    partial_ref[...] = total_ref[...].astype(BF16)
    tau_grad_ref[...] = tau_rows_ref[pl.ds(0, entries.slot_count)]


def push_kernel(entries, distances, table_ref, held_ref, adjoint_ref, partial_ref, total_ref):
    push_entries(entries, distances, table_ref, lambda entry: adjoint_ref[entry], held_ref, total_ref)
    partial_ref[...] = total_ref[...].astype(partial_ref.dtype)


def add_kernel(x_ref, y_ref, out_ref):
    out_ref[...] = (x_ref[...].astype(F32) + y_ref[...].astype(F32)).astype(out_ref.dtype)


def finish_kernel(n, *refs):
    own_sum_ref, received = refs[0], refs[1 : 1 + n]
    io_ref, share_ref, logsum_ref, elasticity_ref, tau_ref, tau_received_ref = refs[1 + n : 7 + n]
    prices_ref, price_grad_ref, wage_grad_ref, tau_grad_ref = refs[7 + n :]
    tau_grad_ref[...] = tau_ref[...].astype(F32) + tau_received_ref[...].astype(F32)
    for r in range(own_sum_ref.shape[0]):
        prices_ref[r] = (-logsum_ref[r] / elasticity_ref[...]).astype(BF16)
        cost_adjoint = own_sum_ref[r]
        for ref in received:
            cost_adjoint = cost_adjoint + ref[r].astype(F32)
        price_grad_ref[r] = lax.dot_general(
            cost_adjoint.astype(BF16), io_ref[r], CONTRACT_LAST, preferred_element_type=F32
        )
        wage_grad_ref[r] = jnp.sum(cost_adjoint * share_ref[pl.ds(r, 1)], axis=1)


def shards(
    log_prices,
    log_wages,
    labor_share,
    io_coeffs,
    pair_blocks,
    log_tau,
    elasticity,
    partners,
    list_lengths,
    price_cotangent,
):
    own, episodes, sectors = log_prices.shape
    slots = pair_blocks.shape[1]
    reg_count = lax.axis_size("reg")
    ep_count = lax.axis_size("ep")
    entries = Entries(own, slots, reg_count)
    blocks = pair_blocks.reshape(own * slots, sectors, sectors)
    row = (episodes, sectors)
    stages = radices(reg_count)

    unit_cost = (
        labor_share[:, None, :] * log_wages[:, :, None]
        + jnp.einsum("iek,ikj->iej", log_prices, io_coeffs, preferred_element_type=F32)
    ).astype(BF16)

    held, tau, cotangent, elastic, cost_copy, table = pl.pallas_call(
        functools.partial(load_kernel, entries),
        out_shape=(
            shape(blocks.shape, BF16),
            shape((own * slots, sectors), F32),
            shape(price_cotangent.shape, F32),
            shape((1, sectors), F32),
            shape(unit_cost.shape, BF16),
            pltpu.SMEM((entries.columns * entries.stride,), jnp.int32),
        ),
        in_specs=[SMEM, VMEM] + [HBM] * 6,
        out_specs=(VMEM,) * 5 + (SMEM,),
        scratch_shapes=[
            pltpu.SMEM(partners.shape, jnp.int32),
            pltpu.SMEM(list_lengths.shape, jnp.int32),
            pltpu.SMEM((reg_count,), jnp.int32),
            pltpu.SemaphoreType.DMA((6,)),
        ],
        compiler_params=params(1),
        cost_estimate=effort(blocks.size),
        name="load",
    )(
        lax.axis_index("reg").reshape(1),
        unit_cost,
        in_hbm(blocks),
        in_hbm(log_tau.reshape(own * slots, sectors)),
        in_hbm(price_cotangent),
        in_hbm(elasticity.reshape(1, sectors)),
        in_hbm(partners),
        in_hbm(list_lengths),
    )

    near, near_distances = [unit_cost], [0]
    stride = reg_count
    for radix in reversed(stages):
        stride //= radix
        whole, distances = jnp.concatenate(near, axis=0), near_distances
        order = [*range(2, radix), 1]
        received = [from_peer(whole, j * stride, "reg", reg_count) for j in order]
        reached = [[d + j * stride for d in distances] for j in order]
        near[0] = cost_copy
        if stride > 1:
            near = near + received
            near_distances = sum(reached, distances)
    far_distances = sum(reached, [])

    def scored(distances):
        return (
            shape((len(distances) * entries.capacity,) + row, F32),
            shape((own + 1,) + row, F32),
            shape((own + 1,) + row, F32),
        )

    radix = stages[0]
    groups = [range(j, reg_count, radix) for j in range(radix)]
    turned = entries.turned(groups[-1])
    held, *near_scores, turned_blocks = pl.pallas_call(
        functools.partial(near_kernel, entries, near_distances, turned, len(near)),
        out_shape=(shape(blocks.shape, BF16),)
        + scored(near_distances)
        + (shape((max(len(turned), 1), sectors, sectors), BF16),),
        in_specs=[SMEM, HBM] + [VMEM] * (3 + len(near)),
        out_specs=(VMEM,) * 5,
        scratch_shapes=[pltpu.SemaphoreType.DMA((own,))],
        input_output_aliases={2: 0},
        compiler_params=params(2),
        cost_estimate=effort(blocks.size),
        name="near",
    )(table, in_hbm(blocks), held, tau, elastic, *near)
    partial_dims = (reg_count // radix * own,) + row
    adjoint, tau_grad, logsum, partial = pl.pallas_call(
        functools.partial(adjoint_kernel, entries, near_distances, far_distances, groups[-1], turned),
        out_shape=(
            shape((entries.count,) + row, BF16),
            shape((own * slots, sectors), F32),
            shape((own,) + row, F32),
            shape(partial_dims, BF16),
        ),
        in_specs=[SMEM] + [VMEM] * (8 + len(received)),
        out_specs=(VMEM,) * 4,
        scratch_shapes=[
            *[pltpu.VMEM(s.shape, F32) for s in scored(far_distances)],
            pltpu.VMEM((2, own + 1) + row, F32),
            pltpu.VMEM((own * slots + 8, sectors), F32),
            pltpu.VMEM(partial_dims, F32),
        ],
        compiler_params=params(8),
        cost_estimate=effort(blocks.size),
        name="adjoint",
    )(table, held, turned_blocks, tau, elastic, cotangent, *near_scores, *received)

    def push(j, dtype):
        return pl.pallas_call(
            functools.partial(push_kernel, entries, groups[j]),
            out_shape=shape(partial_dims, dtype),
            in_specs=[SMEM, VMEM, VMEM],
            out_specs=VMEM,
            scratch_shapes=[pltpu.VMEM(partial_dims, F32)],
            compiler_params=params(8),
            cost_estimate=effort(blocks.size),
            name="push",
        )(table, held, adjoint)

    received = [to_peer(partial, radix - 1, "reg", reg_count)] if radix > 1 else []
    for j in range(radix - 2, 0, -1):
        received.append(to_peer(push(j, BF16), j, "reg", reg_count))
    summed = push(0, F32) if radix > 1 else partial.astype(F32)
    stride = 1
    for following in stages[1:]:
        for block in received:
            summed = summed + block.astype(F32)
        stride *= radix
        radix = following
        parts = summed.reshape((-1, radix, own) + row)
        received = [
            to_peer(parts[:, j].reshape((-1,) + row).astype(BF16), j * stride, "reg", reg_count)
            for j in range(radix - 1, 0, -1)
        ]
        summed = parts[:, 0].reshape((-1,) + row)

    if is_power_of_two(ep_count):
        tau_received = jnp.zeros_like(tau_grad)
        distance = 1
        while distance < ep_count:
            if distance > 1:
                tau_grad = pl.pallas_call(
                    add_kernel,
                    out_shape=shape(tau_grad.shape, F32),
                    in_specs=[VMEM, VMEM],
                    out_specs=VMEM,
                    compiler_params=params(1),
                    cost_estimate=effort(1),
                    name="add",
                )(tau_grad, tau_received)
            tau_received = to_peer(tau_grad, distance, "ep", ep_count)
            distance *= 2
    else:
        tau_grad = lax.psum(tau_grad, "ep")
        tau_received = jnp.zeros_like(tau_grad)

    new_prices, price_grad, wage_grad, tau_grad = pl.pallas_call(
        functools.partial(finish_kernel, len(received)),
        out_shape=(
            shape((own,) + row, BF16),
            shape((own,) + row, F32),
            shape((own, episodes), F32),
            shape(tau_grad.shape, F32),
        ),
        in_specs=[VMEM] * (7 + len(received)),
        out_specs=(VMEM,) * 4,
        compiler_params=params(4),
        name="finish",
    )(summed, *received, io_coeffs, labor_share, logsum, elastic, tau_grad, tau_received)
    return new_prices, price_grad, wage_grad, tau_grad.reshape(own, slots, sectors)


def solution(mesh):
    return jax.shard_map(
        shards,
        mesh=mesh,
        in_specs=(
            P("reg", "ep", None),
            P("reg", "ep"),
            P("reg", None),
            P("reg", None, None),
            P("reg", None, None, None),
            P("reg", None, None),
            P(),
            P(),
            P(),
            P("reg", "ep", None),
        ),
        out_specs=(
            P("reg", "ep", None),
            P("reg", "ep", None),
            P("reg", "ep"),
            P("reg", None, None),
        ),
        check_vma=False,
    )
```

```python
import functools

import jax
import jax.numpy as jnp
from jax import lax
from jax.experimental import pallas as pl
from jax.experimental.pallas import tpu as pltpu
from jax.sharding import PartitionSpec as P

F32 = jnp.float32
BF16 = jnp.bfloat16
CONTRACT_LAST = (((1,), (1,)), ((), ()))
LOWEST = -1e30
VMEM = pl.BlockSpec(memory_space=pltpu.VMEM)
SMEM = pl.BlockSpec(memory_space=pltpu.SMEM)
HBM = pl.BlockSpec(memory_space=pltpu.HBM)


def is_power_of_two(n):
    return n & (n - 1) == 0


def peer(i, distance, n):
    return i ^ distance if is_power_of_two(n) else (i + distance) % n


def distance_of(owner, me, n):
    return owner ^ me if is_power_of_two(n) else lax.rem(owner - me + n, n)


def radices(n):
    stages = []
    if n.bit_length() % 2 == 0 and is_power_of_two(n):
        stages.append(2)
        n //= 2
    while n % 4 == 0:
        stages.append(4)
        n //= 4
    if n > 1 or not stages:
        stages.append(n)
    return stages


def from_peer(x, distance, axis, n):
    return lax.ppermute(x, axis, [(peer(i, distance, n), i) for i in range(n)])


def to_peer(x, distance, axis, n):
    return lax.ppermute(x, axis, [(i, peer(i, distance, n)) for i in range(n)])


def shape(dims, dtype):
    return jax.ShapeDtypeStruct(dims, dtype)


def params(mebibytes):
    return pltpu.CompilerParams(vmem_limit_bytes=mebibytes << 20)


def effort(size):
    return pl.CostEstimate(flops=0, bytes_accessed=size, transcendentals=0)


def in_hbm(x):
    return pltpu.with_memory_space_constraint(x, pltpu.HBM)


class Entries:
    def __init__(self, own, slots, reg_count):
        self.own, self.slots, self.reg_count = own, slots, reg_count
        self.slot_count = own * slots
        self.loaded_first = 4 * own * slots // 8
        self.dense = reg_count * own <= slots
        self.capacity = own * own if self.dense else -(-own * slots // reg_count)
        self.count = self.capacity * reg_count
        self.stride = self.count + 1
        self.columns = 2 if self.dense else 4

    def numbers(self, distances):
        return [distance * self.capacity + i for distance in distances for i in range(self.capacity)]

    def turned(self, distances):
        if not self.dense:
            return []
        return self.numbers(distances)

    def slot(self, table, entry):
        return table[entry]

    def row(self, table, entry):
        return table[self.stride + entry]

    def live(self, table, entry):
        return self.row(table, entry) < self.slot_count

    def importer(self, table, entry):
        return entry % self.capacity // self.own if self.dense else table[2 * self.stride + entry]

    def place(self, table, entry):
        return entry % self.own if self.dense else table[3 * self.stride + entry]

    def fill(self, table, found, partners, lengths, me):
        own = self.own
        for entry in range(self.stride):
            for column, value in enumerate((0, self.slot_count, own, 0)[: self.columns]):
                table[column * self.stride + entry] = value
        if not self.dense:
            for distance in range(self.reg_count):
                found[distance] = 0
        for r in range(own):
            length = lengths[me * own + r]
            for s in range(self.slots):
                partner = partners[me * own + r, s]
                distance = distance_of(lax.div(partner, own), me, self.reg_count)
                place = lax.rem(partner, own)
                slot = r * self.slots + s
                if self.dense:
                    entry = distance * self.capacity + r * own + place
                    columns = (slot, slot)
                else:
                    entry = distance * self.capacity + found[distance]
                    columns = (slot, slot, r, place)
                    found[distance] += (s < length).astype(jnp.int32)
                entry = jnp.minimum(jnp.where(s < length, entry, self.count), self.count)
                for column, value in enumerate(columns):
                    table[column * self.stride + entry] = value


def load_kernel(
    entries, me_ref, cost_ref, blocks, tau, cotangent, elasticity, partners, lengths,
    held_ref, tau_ref, cotangent_ref, elasticity_ref, cost_copy_ref, table_ref,
    partners_ref, lengths_ref, found_ref, sems,
):
    copies = [
        pltpu.make_async_copy(source, target, sems.at[i])
        for i, (source, target) in enumerate(
            (
                (partners, partners_ref),
                (lengths, lengths_ref),
                (tau, tau_ref),
                (cotangent, cotangent_ref),
                (elasticity, elasticity_ref),
                (blocks.at[pl.ds(0, entries.loaded_first)], held_ref.at[pl.ds(0, entries.loaded_first)]),
            )
        )
    ]
    for copy in copies:
        copy.start()
    cost_copy_ref[...] = cost_ref[...]
    copies[0].wait()
    copies[1].wait()
    entries.fill(table_ref, found_ref, partners_ref, lengths_ref, me_ref[0])
    for copy in copies[2:]:
        copy.wait()


def scorer(entries, numbers, table_ref, costs, held_ref, tau_ref, elasticity_ref):
    scale = -elasticity_ref[...]
    rows = [(ref, block) for ref in costs for block in range(ref.shape[0] // entries.own)]

    def score(i):
        entry = numbers[i]
        ref, block = rows[i // entries.capacity]
        slot = entries.slot(table_ref, entry)
        cost = ref[block * entries.own + entries.place(table_ref, entry)]
        landed = jnp.dot(cost, held_ref[slot], preferred_element_type=F32) + tau_ref[pl.ds(slot, 1)]
        value = scale * landed
        return jnp.where(entries.live(table_ref, entry), value, -jnp.inf) if entries.dense else value

    return score


def score_entries(
    entries, distances, table_ref, costs, held_ref, tau_ref, elasticity_ref, weights_ref, top_ref, norm_ref,
    arrive=lambda r: None,
):
    own = entries.own
    numbers = entries.numbers(distances)
    count = len(numbers)
    lowest = jnp.full(top_ref.shape[1:], LOWEST, F32)
    zero = jnp.zeros(top_ref.shape[1:], F32)
    score = scorer(entries, numbers, table_ref, costs, held_ref, tau_ref, elasticity_ref)
    if entries.dense:
        for r in range(own):
            arrive(r)
            members = [i for i in range(count) if entries.importer(table_ref, numbers[i]) == r]
            scores = [score(i) for i in members]
            top = functools.reduce(jnp.maximum, scores, lowest)
            norm = zero
            for i, value in zip(members, scores):
                weight = jnp.exp(value - top)
                weights_ref[i] = weight
                norm = norm + weight
            top_ref[r] = top
            norm_ref[r] = norm
        return
    arrive(None)
    top_ref[...] = jnp.full(top_ref.shape, LOWEST, F32)
    norm_ref[...] = jnp.zeros(norm_ref.shape, F32)
    for i in range(count):
        importer = entries.importer(table_ref, numbers[i])
        value = score(i)
        weights_ref[i] = value
        top_ref[importer] = jnp.maximum(top_ref[importer], value)
    for i in range(count):
        importer = entries.importer(table_ref, numbers[i])
        weight = jnp.exp(weights_ref[i] - top_ref[importer])
        weights_ref[i] = weight
        norm_ref[importer] += weight


def near_kernel(entries, distances, turned, n_costs, *refs):
    table_ref, blocks, _, tau_ref, elasticity_ref = refs[:5]
    costs = refs[5 : 5 + n_costs]
    held_ref, weights_ref, top_ref, norm_ref, turned_ref, sems = refs[5 + n_costs :]
    copies = []
    for r in range(entries.own):
        start, stop = max(r * entries.slots, entries.loaded_first), (r + 1) * entries.slots
        if start < stop:
            part = pl.ds(start, stop - start)
            copies.append(pltpu.make_async_copy(blocks.at[part], held_ref.at[part], sems.at[r]))
    for copy in copies:
        copy.start()
    skipped = entries.own - len(copies)

    def arrive(r):
        for copy in copies if r is None else copies[r - skipped : r - skipped + 1] if r >= skipped else []:
            copy.wait()
        for i, entry in enumerate(turned):
            if r is None or entries.importer(table_ref, entry) == r:
                turned_ref[i] = held_ref[entries.slot(table_ref, entry)].T

    score_entries(
        entries, distances, table_ref, costs, held_ref, tau_ref, elasticity_ref, weights_ref, top_ref, norm_ref, arrive
    )


def push_entries(entries, distances, table_ref, adjoint_of, held_ref, total_ref):
    own, capacity = entries.own, entries.capacity

    def pushed(entry):
        return lax.dot_general(
            adjoint_of(entry),
            held_ref[entries.slot(table_ref, entry)],
            CONTRACT_LAST,
            preferred_element_type=F32,
        )

    if entries.dense:
        for block, distance in enumerate(distances):
            for place in range(own):
                terms = [pushed(distance * capacity + r * own + place) for r in range(own)]
                total_ref[block * own + place] = sum(terms[1:], terms[0]).astype(total_ref.dtype)
        return
    total_ref[...] = jnp.zeros(total_ref.shape, total_ref.dtype)
    for block, distance in enumerate(distances):
        for entry in range(distance * capacity, (distance + 1) * capacity):
            total_ref[block * own + entries.place(table_ref, entry)] += pushed(entry)


def adjoint_kernel(entries, near_distances, far_distances, group, turned, *refs):
    table_ref, held_ref, turned_ref, tau_ref, elasticity_ref, cotangent_ref, near_weights, near_top, near_norm = refs[:9]
    costs = refs[9:-10]
    adjoint_ref, tau_grad_ref, logsum_ref, partial_ref = refs[-10:-6]
    far_weights, far_top, far_norm, factor_ref, tau_rows_ref, total_ref = refs[-6:]
    own, capacity = entries.own, entries.capacity
    near, far = entries.numbers(near_distances), entries.numbers(far_distances)
    tau_rows_ref[...] = jnp.zeros(tau_rows_ref.shape, F32)

    def rounded(entry, value):
        tau_rows_ref[pl.ds(entries.row(table_ref, entry), 1)] = jnp.sum(value, axis=0, keepdims=True)
        return value.astype(BF16)

    def pushed(entry, value):
        if entry in turned:
            return jnp.dot(value, turned_ref[turned.index(entry)], preferred_element_type=F32)
        return lax.dot_general(
            value, held_ref[entries.slot(table_ref, entry)], CONTRACT_LAST, preferred_element_type=F32
        )

    if entries.dense:
        score = scorer(entries, far, table_ref, costs, held_ref, tau_ref, elasticity_ref)
        members = [[i for i, entry in enumerate(far) if entries.importer(None, entry) == r] for r in range(own)]

        def emit(r, entry, value):
            value = rounded(entry, value)
            if entry // capacity not in group:
                adjoint_ref[entry] = value
                return
            place = group.index(entry // capacity) * own + entries.place(None, entry)
            term = pushed(entry, value)
            total_ref[place] = term if r == 0 else total_ref[place] + term

        for r in range(own + 1):
            if r < own:
                for i in members[r]:
                    far_weights[i] = score(i)
            if r == 0:
                continue
            q = r - 1
            top = functools.reduce(jnp.maximum, [far_weights[i] for i in members[q]], near_top[q])
            weights = [jnp.exp(far_weights[i] - top) for i in members[q]]
            shrink = jnp.exp(near_top[q] - top)
            norm = sum(weights, near_norm[q] * shrink)
            logsum_ref[q] = top + jnp.log(norm)
            scale = cotangent_ref[q] / norm
            for i, weight in zip(members[q], weights):
                emit(q, far[i], scale * weight)
            scale = scale * shrink
            for i, entry in enumerate(near):
                if entries.importer(None, entry) == q:
                    emit(q, entry, scale * near_weights[i])
    else:
        score_entries(
            entries, far_distances, table_ref, costs, held_ref, tau_ref, elasticity_ref, far_weights, far_top, far_norm
        )
        for r in range(own):
            top = jnp.maximum(near_top[r], far_top[r])
            shrink = [jnp.exp(near_top[r] - top), jnp.exp(far_top[r] - top)]
            norm = near_norm[r] * shrink[0] + far_norm[r] * shrink[1]
            logsum_ref[r] = top + jnp.log(norm)
            for k in range(2):
                factor_ref[k, r] = cotangent_ref[r] / norm * shrink[k]
        for k in range(2):
            factor_ref[k, own] = jnp.zeros(factor_ref.shape[2:], F32)
        total_ref[...] = jnp.zeros(total_ref.shape, F32)
        for k, (numbers, weights_ref) in enumerate(((near, near_weights), (far, far_weights))):
            for i, entry in enumerate(numbers):
                value = rounded(entry, factor_ref[k, entries.importer(table_ref, entry)] * weights_ref[i])
                if entry // capacity in group:
                    place = group.index(entry // capacity) * own + entries.place(table_ref, entry)
                    total_ref[place] += pushed(entry, value)
                else:
                    adjoint_ref[entry] = value
    partial_ref[...] = total_ref[...].astype(BF16)
    tau_grad_ref[...] = tau_rows_ref[pl.ds(0, entries.slot_count)].astype(tau_grad_ref.dtype)


def push_kernel(entries, distances, table_ref, held_ref, adjoint_ref, partial_ref, total_ref):
    push_entries(entries, distances, table_ref, lambda entry: adjoint_ref[entry], held_ref, total_ref)
    partial_ref[...] = total_ref[...].astype(partial_ref.dtype)


def add_kernel(x_ref, y_ref, out_ref):
    out_ref[...] = (x_ref[...].astype(F32) + y_ref[...].astype(F32)).astype(out_ref.dtype)


def finish_kernel(n, *refs):
    own_sum_ref, received = refs[0], refs[1 : 1 + n]
    io_ref, share_ref, logsum_ref, elasticity_ref, tau_ref, tau_received_ref = refs[1 + n : 7 + n]
    prices_ref, price_grad_ref, wage_grad_ref, tau_grad_ref = refs[7 + n :]
    tau_grad_ref[...] = tau_ref[...].astype(F32) + tau_received_ref[...].astype(F32)
    for r in range(own_sum_ref.shape[0]):
        prices_ref[r] = (-logsum_ref[r] / elasticity_ref[...]).astype(BF16)
        cost_adjoint = own_sum_ref[r]
        for ref in received:
            cost_adjoint = cost_adjoint + ref[r].astype(F32)
        price_grad_ref[r] = lax.dot_general(
            cost_adjoint.astype(BF16), io_ref[r], CONTRACT_LAST, preferred_element_type=F32
        )
        wage_grad_ref[r] = jnp.sum(cost_adjoint * share_ref[pl.ds(r, 1)], axis=1)


def shards(
    log_prices,
    log_wages,
    labor_share,
    io_coeffs,
    pair_blocks,
    log_tau,
    elasticity,
    partners,
    list_lengths,
    price_cotangent,
):
    own, episodes, sectors = log_prices.shape
    slots = pair_blocks.shape[1]
    reg_count = lax.axis_size("reg")
    ep_count = lax.axis_size("ep")
    entries = Entries(own, slots, reg_count)
    blocks = pair_blocks.reshape(own * slots, sectors, sectors)
    row = (episodes, sectors)
    stages = radices(reg_count)

    unit_cost = (
        labor_share[:, None, :] * log_wages[:, :, None]
        + jnp.einsum("iek,ikj->iej", log_prices, io_coeffs, preferred_element_type=F32)
    ).astype(BF16)

    held, tau, cotangent, elastic, cost_copy, table = pl.pallas_call(
        functools.partial(load_kernel, entries),
        out_shape=(
            shape(blocks.shape, BF16),
            shape((own * slots, sectors), F32),
            shape(price_cotangent.shape, F32),
            shape((1, sectors), F32),
            shape(unit_cost.shape, BF16),
            pltpu.SMEM((entries.columns * entries.stride,), jnp.int32),
        ),
        in_specs=[SMEM, VMEM] + [HBM] * 6,
        out_specs=(VMEM,) * 5 + (SMEM,),
        scratch_shapes=[
            pltpu.SMEM(partners.shape, jnp.int32),
            pltpu.SMEM(list_lengths.shape, jnp.int32),
            pltpu.SMEM((reg_count,), jnp.int32),
            pltpu.SemaphoreType.DMA((6,)),
        ],
        compiler_params=params(1),
        cost_estimate=effort(blocks.size),
        name="load",
    )(
        lax.axis_index("reg").reshape(1),
        unit_cost,
        in_hbm(blocks),
        in_hbm(log_tau.reshape(own * slots, sectors)),
        in_hbm(price_cotangent),
        in_hbm(elasticity.reshape(1, sectors)),
        in_hbm(partners),
        in_hbm(list_lengths),
    )

    near, near_distances = [unit_cost], [0]
    stride = reg_count
    for radix in reversed(stages):
        stride //= radix
        whole, distances = jnp.concatenate(near, axis=0), near_distances
        order = [*range(2, radix), 1]
        received = [from_peer(whole, j * stride, "reg", reg_count) for j in order]
        reached = [[d + j * stride for d in distances] for j in order]
        near[0] = cost_copy
        if stride > 1:
            near = near + received
            near_distances = sum(reached, distances)
    far_distances = sum(reached, [])

    def scored(distances):
        return (
            shape((len(distances) * entries.capacity,) + row, F32),
            shape((own + 1,) + row, F32),
            shape((own + 1,) + row, F32),
        )

    radix = stages[0]
    groups = [range(j, reg_count, radix) for j in range(radix)]
    turned = entries.turned(groups[-1])
    held, *near_scores, turned_blocks = pl.pallas_call(
        functools.partial(near_kernel, entries, near_distances, turned, len(near)),
        out_shape=(shape(blocks.shape, BF16),)
        + scored(near_distances)
        + (shape((max(len(turned), 1), sectors, sectors), BF16),),
        in_specs=[SMEM, HBM] + [VMEM] * (3 + len(near)),
        out_specs=(VMEM,) * 5,
        scratch_shapes=[pltpu.SemaphoreType.DMA((own,))],
        input_output_aliases={2: 0},
        compiler_params=params(2),
        cost_estimate=effort(blocks.size),
        name="near",
    )(table, in_hbm(blocks), held, tau, elastic, *near)
    partial_dims = (reg_count // radix * own,) + row
    adjoint, tau_grad, logsum, partial = pl.pallas_call(
        functools.partial(adjoint_kernel, entries, near_distances, far_distances, groups[-1], turned),
        out_shape=(
            shape((entries.count,) + row, BF16),
            shape((own * slots, sectors), BF16),
            shape((own,) + row, F32),
            shape(partial_dims, BF16),
        ),
        in_specs=[SMEM] + [VMEM] * (8 + len(received)),
        out_specs=(VMEM,) * 4,
        scratch_shapes=[
            *[pltpu.VMEM(s.shape, F32) for s in scored(far_distances)],
            pltpu.VMEM((2, own + 1) + row, F32),
            pltpu.VMEM((own * slots + 8, sectors), F32),
            pltpu.VMEM(partial_dims, F32),
        ],
        compiler_params=params(8),
        cost_estimate=effort(blocks.size),
        name="adjoint",
    )(table, held, turned_blocks, tau, elastic, cotangent, *near_scores, *received)

    def push(j, dtype):
        return pl.pallas_call(
            functools.partial(push_kernel, entries, groups[j]),
            out_shape=shape(partial_dims, dtype),
            in_specs=[SMEM, VMEM, VMEM],
            out_specs=VMEM,
            scratch_shapes=[pltpu.VMEM(partial_dims, F32)],
            compiler_params=params(8),
            cost_estimate=effort(blocks.size),
            name="push",
        )(table, held, adjoint)

    received = [to_peer(partial, radix - 1, "reg", reg_count)] if radix > 1 else []
    for j in range(radix - 2, 0, -1):
        received.append(to_peer(push(j, BF16), j, "reg", reg_count))
    summed = push(0, F32) if radix > 1 else partial.astype(F32)
    stride = 1
    for following in stages[1:]:
        for block in received:
            summed = summed + block.astype(F32)
        stride *= radix
        radix = following
        parts = summed.reshape((-1, radix, own) + row)
        received = [
            to_peer(parts[:, j].reshape((-1,) + row).astype(BF16), j * stride, "reg", reg_count)
            for j in range(radix - 1, 0, -1)
        ]
        summed = parts[:, 0].reshape((-1,) + row)

    if is_power_of_two(ep_count):
        tau_received = jnp.zeros_like(tau_grad)
        distance = 1
        while distance < ep_count:
            if distance > 1:
                tau_grad = pl.pallas_call(
                    add_kernel,
                    out_shape=shape(tau_grad.shape, F32),
                    in_specs=[VMEM, VMEM],
                    out_specs=VMEM,
                    compiler_params=params(1),
                    cost_estimate=effort(1),
                    name="add",
                )(tau_grad, tau_received)
            tau_received = to_peer(tau_grad, distance, "ep", ep_count)
            distance *= 2
    else:
        tau_grad = lax.psum(tau_grad.astype(F32), "ep")
        tau_received = jnp.zeros_like(tau_grad)

    new_prices, price_grad, wage_grad, tau_grad = pl.pallas_call(
        functools.partial(finish_kernel, len(received)),
        out_shape=(
            shape((own,) + row, BF16),
            shape((own,) + row, F32),
            shape((own, episodes), F32),
            shape(tau_grad.shape, F32),
        ),
        in_specs=[VMEM] * (7 + len(received)),
        out_specs=(VMEM,) * 4,
        compiler_params=params(4),
        name="finish",
    )(summed, *received, io_coeffs, labor_share, logsum, elastic, tau_grad, tau_received)
    return new_prices, price_grad, wage_grad, tau_grad.reshape(own, slots, sectors)


def solution(mesh):
    return jax.shard_map(
        shards,
        mesh=mesh,
        in_specs=(
            P("reg", "ep", None),
            P("reg", "ep"),
            P("reg", None),
            P("reg", None, None),
            P("reg", None, None, None),
            P("reg", None, None),
            P(),
            P(),
            P(),
            P("reg", "ep", None),
        ),
        out_specs=(
            P("reg", "ep", None),
            P("reg", "ep", None),
            P("reg", "ep"),
            P("reg", None, None),
        ),
        check_vma=False,
    )
```

```python
import functools

import jax
import jax.numpy as jnp
from jax import lax
from jax.experimental import pallas as pl
from jax.experimental.pallas import tpu as pltpu
from jax.sharding import PartitionSpec as P

F32 = jnp.float32
BF16 = jnp.bfloat16
CONTRACT_LAST = (((1,), (1,)), ((), ()))
LOWEST = -1e30
VMEM = pl.BlockSpec(memory_space=pltpu.VMEM)
SMEM = pl.BlockSpec(memory_space=pltpu.SMEM)
HBM = pl.BlockSpec(memory_space=pltpu.HBM)


def is_power_of_two(n):
    return n & (n - 1) == 0


def peer(i, distance, n):
    return i ^ distance if is_power_of_two(n) else (i + distance) % n


def distance_of(owner, me, n):
    return owner ^ me if is_power_of_two(n) else lax.rem(owner - me + n, n)


def radices(n):
    stages = []
    if n.bit_length() % 2 == 0 and is_power_of_two(n):
        stages.append(2)
        n //= 2
    while n % 4 == 0:
        stages.append(4)
        n //= 4
    if n > 1 or not stages:
        stages.append(n)
    return stages


def from_peer(x, distance, axis, n):
    return lax.ppermute(x, axis, [(peer(i, distance, n), i) for i in range(n)])


def to_peer(x, distance, axis, n):
    return lax.ppermute(x, axis, [(i, peer(i, distance, n)) for i in range(n)])


def shape(dims, dtype):
    return jax.ShapeDtypeStruct(dims, dtype)


def params(mebibytes):
    return pltpu.CompilerParams(vmem_limit_bytes=mebibytes << 20)


def effort(size):
    return pl.CostEstimate(flops=0, bytes_accessed=size, transcendentals=0)


def in_hbm(x):
    return pltpu.with_memory_space_constraint(x, pltpu.HBM)


class Entries:
    def __init__(self, own, slots, reg_count):
        self.own, self.slots, self.reg_count = own, slots, reg_count
        self.slot_count = own * slots
        self.loaded_first = 4 * own * slots // 8
        self.dense = reg_count * own <= slots
        self.capacity = own * own if self.dense else -(-own * slots // reg_count)
        self.count = self.capacity * reg_count
        self.stride = self.count + 1
        self.columns = 2 if self.dense else 4

    def numbers(self, distances):
        return [distance * self.capacity + i for distance in distances for i in range(self.capacity)]

    def turned(self, distances):
        if not self.dense:
            return []
        return [entry for entry in self.numbers(distances) if self.importer(None, entry) < max(self.own - 1, 1)]

    def slot(self, table, entry):
        return table[entry]

    def row(self, table, entry):
        return table[self.stride + entry]

    def live(self, table, entry):
        return self.row(table, entry) < self.slot_count

    def importer(self, table, entry):
        return entry % self.capacity // self.own if self.dense else table[2 * self.stride + entry]

    def place(self, table, entry):
        return entry % self.own if self.dense else table[3 * self.stride + entry]

    def fill(self, table, found, partners, lengths, me):
        own = self.own
        for entry in range(self.stride):
            for column, value in enumerate((0, self.slot_count, own, 0)[: self.columns]):
                table[column * self.stride + entry] = value
        if not self.dense:
            for distance in range(self.reg_count):
                found[distance] = 0
        for r in range(own):
            length = lengths[me * own + r]
            for s in range(self.slots):
                partner = partners[me * own + r, s]
                distance = distance_of(lax.div(partner, own), me, self.reg_count)
                place = lax.rem(partner, own)
                slot = r * self.slots + s
                if self.dense:
                    entry = distance * self.capacity + r * own + place
                    columns = (slot, slot)
                else:
                    entry = distance * self.capacity + found[distance]
                    columns = (slot, slot, r, place)
                    found[distance] += (s < length).astype(jnp.int32)
                entry = jnp.minimum(jnp.where(s < length, entry, self.count), self.count)
                for column, value in enumerate(columns):
                    table[column * self.stride + entry] = value


def load_kernel(
    entries, me_ref, cost_ref, blocks, tau, cotangent, elasticity, partners, lengths,
    held_ref, tau_ref, cotangent_ref, elasticity_ref, cost_copy_ref, table_ref,
    partners_ref, lengths_ref, found_ref, sems,
):
    copies = [
        pltpu.make_async_copy(source, target, sems.at[i])
        for i, (source, target) in enumerate(
            (
                (partners, partners_ref),
                (lengths, lengths_ref),
                (tau, tau_ref),
                (cotangent, cotangent_ref),
                (elasticity, elasticity_ref),
                (blocks.at[pl.ds(0, entries.loaded_first)], held_ref.at[pl.ds(0, entries.loaded_first)]),
            )
        )
    ]
    for copy in copies:
        copy.start()
    cost_copy_ref[...] = cost_ref[...]
    copies[0].wait()
    copies[1].wait()
    entries.fill(table_ref, found_ref, partners_ref, lengths_ref, me_ref[0])
    for copy in copies[2:]:
        copy.wait()


def scorer(entries, numbers, table_ref, costs, held_ref, tau_ref, elasticity_ref):
    scale = -elasticity_ref[...]
    rows = [(ref, block) for ref in costs for block in range(ref.shape[0] // entries.own)]

    def score(i):
        entry = numbers[i]
        ref, block = rows[i // entries.capacity]
        slot = entries.slot(table_ref, entry)
        cost = ref[block * entries.own + entries.place(table_ref, entry)]
        landed = jnp.dot(cost, held_ref[slot], preferred_element_type=F32) + tau_ref[pl.ds(slot, 1)]
        value = scale * landed
        return jnp.where(entries.live(table_ref, entry), value, -jnp.inf) if entries.dense else value

    return score


def score_entries(
    entries, distances, table_ref, costs, held_ref, tau_ref, elasticity_ref, weights_ref, top_ref, norm_ref,
    arrive=lambda r: None,
):
    own = entries.own
    numbers = entries.numbers(distances)
    count = len(numbers)
    lowest = jnp.full(top_ref.shape[1:], LOWEST, F32)
    zero = jnp.zeros(top_ref.shape[1:], F32)
    score = scorer(entries, numbers, table_ref, costs, held_ref, tau_ref, elasticity_ref)
    if entries.dense:
        for r in range(own):
            arrive(r)
            members = [i for i in range(count) if entries.importer(table_ref, numbers[i]) == r]
            scores = [score(i) for i in members]
            top = functools.reduce(jnp.maximum, scores, lowest)
            norm = zero
            for i, value in zip(members, scores):
                weight = jnp.exp(value - top)
                weights_ref[i] = weight
                norm = norm + weight
            top_ref[r] = top
            norm_ref[r] = norm
        return
    arrive(None)
    top_ref[...] = jnp.full(top_ref.shape, LOWEST, F32)
    norm_ref[...] = jnp.zeros(norm_ref.shape, F32)
    for i in range(count):
        importer = entries.importer(table_ref, numbers[i])
        value = score(i)
        weights_ref[i] = value
        top_ref[importer] = jnp.maximum(top_ref[importer], value)
    for i in range(count):
        importer = entries.importer(table_ref, numbers[i])
        weight = jnp.exp(weights_ref[i] - top_ref[importer])
        weights_ref[i] = weight
        norm_ref[importer] += weight


def near_kernel(entries, distances, turned, n_costs, *refs):
    table_ref, blocks, _, tau_ref, elasticity_ref = refs[:5]
    costs = refs[5 : 5 + n_costs]
    held_ref, weights_ref, top_ref, norm_ref, turned_ref, sems = refs[5 + n_costs :]
    copies = []
    for r in range(entries.own):
        start, stop = max(r * entries.slots, entries.loaded_first), (r + 1) * entries.slots
        if start < stop:
            part = pl.ds(start, stop - start)
            copies.append(pltpu.make_async_copy(blocks.at[part], held_ref.at[part], sems.at[r]))
    for copy in copies:
        copy.start()
    skipped = entries.own - len(copies)

    def arrive(r):
        for copy in copies if r is None else copies[r - skipped : r - skipped + 1] if r >= skipped else []:
            copy.wait()
        for i, entry in enumerate(turned):
            if r is None or entries.importer(table_ref, entry) == r:
                turned_ref[i] = held_ref[entries.slot(table_ref, entry)].T

    score_entries(
        entries, distances, table_ref, costs, held_ref, tau_ref, elasticity_ref, weights_ref, top_ref, norm_ref, arrive
    )


def push_entries(entries, distances, table_ref, adjoint_of, held_ref, total_ref, turned_ref):
    own, capacity = entries.own, entries.capacity

    def pushed(entry):
        if entry in turned:
            return jnp.dot(adjoint_of(entry), turned_ref[turned.index(entry)], preferred_element_type=F32)
        return lax.dot_general(
            adjoint_of(entry),
            held_ref[entries.slot(table_ref, entry)],
            CONTRACT_LAST,
            preferred_element_type=F32,
        )

    turned = []
    if entries.dense:
        turned = [entry for entry in entries.numbers(distances) if entries.importer(None, entry) < own // 2]
        for block, distance in enumerate(distances):
            for place in range(own):
                for r in range(own // 2):
                    entry = distance * capacity + r * own + place
                    turned_ref[turned.index(entry)] = held_ref[entries.slot(table_ref, entry)].T
                terms = [pushed(distance * capacity + r * own + place) for r in range(own)]
                total_ref[block * own + place] = sum(terms[1:], terms[0]).astype(total_ref.dtype)
        return
    total_ref[...] = jnp.zeros(total_ref.shape, total_ref.dtype)
    for block, distance in enumerate(distances):
        for entry in range(distance * capacity, (distance + 1) * capacity):
            total_ref[block * own + entries.place(table_ref, entry)] += pushed(entry)


def adjoint_kernel(entries, near_distances, far_distances, group, turned, *refs):
    table_ref, held_ref, turned_ref, tau_ref, elasticity_ref, cotangent_ref, near_weights, near_top, near_norm = refs[:9]
    costs = refs[9:-11]
    adjoint_ref, tau_grad_ref, logsum_ref, partial_ref = refs[-11:-7]
    far_weights, far_top, far_norm, factor_ref, tau_rows_ref, total_ref, late_ref = refs[-7:]
    late = [entry for entry in entries.numbers(group) if entry not in turned] if entries.dense else []
    own, capacity = entries.own, entries.capacity
    near, far = entries.numbers(near_distances), entries.numbers(far_distances)
    tau_rows_ref[...] = jnp.zeros(tau_rows_ref.shape, F32)

    def rounded(entry, value):
        tau_rows_ref[pl.ds(entries.row(table_ref, entry), 1)] = jnp.sum(value, axis=0, keepdims=True)
        return value.astype(BF16)

    def pushed(entry, value):
        if entry in turned:
            return jnp.dot(value, turned_ref[turned.index(entry)], preferred_element_type=F32)
        if entry in late:
            return jnp.dot(value, late_ref[late.index(entry)], preferred_element_type=F32)
        return lax.dot_general(
            value, held_ref[entries.slot(table_ref, entry)], CONTRACT_LAST, preferred_element_type=F32
        )

    if entries.dense:
        score = scorer(entries, far, table_ref, costs, held_ref, tau_ref, elasticity_ref)
        members = [[i for i, entry in enumerate(far) if entries.importer(None, entry) == r] for r in range(own)]

        def emit(r, entry, value):
            value = rounded(entry, value)
            if entry // capacity not in group:
                adjoint_ref[entry] = value
                return
            place = group.index(entry // capacity) * own + entries.place(None, entry)
            term = pushed(entry, value)
            total_ref[place] = term if r == 0 else total_ref[place] + term

        for r in range(own + 1):
            if r < own:
                for i in members[r]:
                    far_weights[i] = score(i)
                for i, entry in enumerate(late):
                    if r == own // 2:
                        late_ref[i] = held_ref[entries.slot(table_ref, entry)].T
            if r == 0:
                continue
            q = r - 1
            top = functools.reduce(jnp.maximum, [far_weights[i] for i in members[q]], near_top[q])
            weights = [jnp.exp(far_weights[i] - top) for i in members[q]]
            shrink = jnp.exp(near_top[q] - top)
            norm = sum(weights, near_norm[q] * shrink)
            logsum_ref[q] = top + jnp.log(norm)
            scale = cotangent_ref[q] / norm
            for i, weight in zip(members[q], weights):
                emit(q, far[i], scale * weight)
            scale = scale * shrink
            for i, entry in enumerate(near):
                if entries.importer(None, entry) == q:
                    emit(q, entry, scale * near_weights[i])
    else:
        score_entries(
            entries, far_distances, table_ref, costs, held_ref, tau_ref, elasticity_ref, far_weights, far_top, far_norm
        )
        for r in range(own):
            top = jnp.maximum(near_top[r], far_top[r])
            shrink = [jnp.exp(near_top[r] - top), jnp.exp(far_top[r] - top)]
            norm = near_norm[r] * shrink[0] + far_norm[r] * shrink[1]
            logsum_ref[r] = top + jnp.log(norm)
            for k in range(2):
                factor_ref[k, r] = cotangent_ref[r] / norm * shrink[k]
        for k in range(2):
            factor_ref[k, own] = jnp.zeros(factor_ref.shape[2:], F32)
        total_ref[...] = jnp.zeros(total_ref.shape, F32)
        for k, (numbers, weights_ref) in enumerate(((near, near_weights), (far, far_weights))):
            for i, entry in enumerate(numbers):
                value = rounded(entry, factor_ref[k, entries.importer(table_ref, entry)] * weights_ref[i])
                if entry // capacity in group:
                    place = group.index(entry // capacity) * own + entries.place(table_ref, entry)
                    total_ref[place] += pushed(entry, value)
                else:
                    adjoint_ref[entry] = value
    partial_ref[...] = total_ref[...].astype(BF16)
    tau_grad_ref[...] = tau_rows_ref[pl.ds(0, entries.slot_count)].astype(tau_grad_ref.dtype)


def push_kernel(entries, distances, table_ref, held_ref, adjoint_ref, partial_ref, total_ref, turned_ref):
    push_entries(entries, distances, table_ref, lambda entry: adjoint_ref[entry], held_ref, total_ref, turned_ref)
    partial_ref[...] = total_ref[...].astype(partial_ref.dtype)


def add_kernel(x_ref, y_ref, out_ref):
    out_ref[...] = (x_ref[...].astype(F32) + y_ref[...].astype(F32)).astype(out_ref.dtype)


def finish_kernel(n, *refs):
    own_sum_ref, received = refs[0], refs[1 : 1 + n]
    io_ref, share_ref, logsum_ref, elasticity_ref, tau_ref, tau_received_ref = refs[1 + n : 7 + n]
    prices_ref, price_grad_ref, wage_grad_ref, tau_grad_ref = refs[7 + n :]
    tau_grad_ref[...] = tau_ref[...].astype(F32) + tau_received_ref[...].astype(F32)
    for r in range(own_sum_ref.shape[0]):
        prices_ref[r] = (-logsum_ref[r] / elasticity_ref[...]).astype(BF16)
        cost_adjoint = own_sum_ref[r]
        for ref in received:
            cost_adjoint = cost_adjoint + ref[r].astype(F32)
        price_grad_ref[r] = lax.dot_general(
            cost_adjoint.astype(BF16), io_ref[r], CONTRACT_LAST, preferred_element_type=F32
        )
        wage_grad_ref[r] = jnp.sum(cost_adjoint * share_ref[pl.ds(r, 1)], axis=1)


def shards(
    log_prices,
    log_wages,
    labor_share,
    io_coeffs,
    pair_blocks,
    log_tau,
    elasticity,
    partners,
    list_lengths,
    price_cotangent,
):
    own, episodes, sectors = log_prices.shape
    slots = pair_blocks.shape[1]
    reg_count = lax.axis_size("reg")
    ep_count = lax.axis_size("ep")
    entries = Entries(own, slots, reg_count)
    blocks = pair_blocks.reshape(own * slots, sectors, sectors)
    row = (episodes, sectors)
    stages = radices(reg_count)

    unit_cost = (
        labor_share[:, None, :] * log_wages[:, :, None]
        + jnp.einsum("iek,ikj->iej", log_prices, io_coeffs, preferred_element_type=F32)
    ).astype(BF16)

    held, tau, cotangent, elastic, cost_copy, table = pl.pallas_call(
        functools.partial(load_kernel, entries),
        out_shape=(
            shape(blocks.shape, BF16),
            shape((own * slots, sectors), F32),
            shape(price_cotangent.shape, F32),
            shape((1, sectors), F32),
            shape(unit_cost.shape, BF16),
            pltpu.SMEM((entries.columns * entries.stride,), jnp.int32),
        ),
        in_specs=[SMEM, VMEM] + [HBM] * 6,
        out_specs=(VMEM,) * 5 + (SMEM,),
        scratch_shapes=[
            pltpu.SMEM(partners.shape, jnp.int32),
            pltpu.SMEM(list_lengths.shape, jnp.int32),
            pltpu.SMEM((reg_count,), jnp.int32),
            pltpu.SemaphoreType.DMA((6,)),
        ],
        compiler_params=params(1),
        cost_estimate=effort(blocks.size),
        name="load",
    )(
        lax.axis_index("reg").reshape(1),
        unit_cost,
        in_hbm(blocks),
        in_hbm(log_tau.reshape(own * slots, sectors)),
        in_hbm(price_cotangent),
        in_hbm(elasticity.reshape(1, sectors)),
        in_hbm(partners),
        in_hbm(list_lengths),
    )

    near, near_distances = [unit_cost], [0]
    stride = reg_count
    for radix in reversed(stages):
        stride //= radix
        whole, distances = jnp.concatenate(near, axis=0), near_distances
        order = [*range(2, radix), 1]
        received = [from_peer(whole, j * stride, "reg", reg_count) for j in order]
        reached = [[d + j * stride for d in distances] for j in order]
        near[0] = cost_copy
        if stride > 1:
            near = near + received
            near_distances = sum(reached, distances)
    far_distances = sum(reached, [])

    def scored(distances):
        return (
            shape((len(distances) * entries.capacity,) + row, F32),
            shape((own + 1,) + row, F32),
            shape((own + 1,) + row, F32),
        )

    radix = stages[0]
    groups = [range(j, reg_count, radix) for j in range(radix)]
    turned = entries.turned(groups[-1])
    held, *near_scores, turned_blocks = pl.pallas_call(
        functools.partial(near_kernel, entries, near_distances, turned, len(near)),
        out_shape=(shape(blocks.shape, BF16),)
        + scored(near_distances)
        + (shape((max(len(turned), 1), sectors, sectors), BF16),),
        in_specs=[SMEM, HBM] + [VMEM] * (3 + len(near)),
        out_specs=(VMEM,) * 5,
        scratch_shapes=[pltpu.SemaphoreType.DMA((own,))],
        input_output_aliases={2: 0},
        compiler_params=params(2),
        cost_estimate=effort(blocks.size),
        name="near",
    )(table, in_hbm(blocks), held, tau, elastic, *near)
    partial_dims = (reg_count // radix * own,) + row
    adjoint, tau_grad, logsum, partial = pl.pallas_call(
        functools.partial(adjoint_kernel, entries, near_distances, far_distances, groups[-1], turned),
        out_shape=(
            shape((entries.count,) + row, BF16),
            shape((own * slots, sectors), BF16),
            shape((own,) + row, F32),
            shape(partial_dims, BF16),
        ),
        in_specs=[SMEM] + [VMEM] * (8 + len(received)),
        out_specs=(VMEM,) * 4,
        scratch_shapes=[
            *[pltpu.VMEM(s.shape, F32) for s in scored(far_distances)],
            pltpu.VMEM((2, own + 1) + row, F32),
            pltpu.VMEM((own * slots + 8, sectors), F32),
            pltpu.VMEM(partial_dims, F32),
            pltpu.VMEM((max((len(groups[-1]) * entries.capacity - len(turned)) * entries.dense, 1), sectors, sectors), BF16),
        ],
        compiler_params=params(16),
        cost_estimate=effort(blocks.size),
        name="adjoint",
    )(table, held, turned_blocks, tau, elastic, cotangent, *near_scores, *received)

    def push(j, dtype):
        return pl.pallas_call(
            functools.partial(push_kernel, entries, groups[j]),
            out_shape=shape(partial_dims, dtype),
            in_specs=[SMEM, VMEM, VMEM],
            out_specs=VMEM,
            scratch_shapes=[
                pltpu.VMEM(partial_dims, F32),
                pltpu.VMEM((max(len(groups[j]) * own * (own // 2) * entries.dense, 1), sectors, sectors), BF16),
            ],
            compiler_params=params(16),
            cost_estimate=effort(blocks.size),
            name="push",
        )(table, held, adjoint)

    received = [to_peer(partial, radix - 1, "reg", reg_count)] if radix > 1 else []
    for j in range(radix - 2, 0, -1):
        received.append(to_peer(push(j, BF16), j, "reg", reg_count))
    summed = push(0, F32) if radix > 1 else partial.astype(F32)
    stride = 1
    for following in stages[1:]:
        for block in received:
            summed = summed + block.astype(F32)
        stride *= radix
        radix = following
        parts = summed.reshape((-1, radix, own) + row)
        received = [
            to_peer(parts[:, j].reshape((-1,) + row).astype(BF16), j * stride, "reg", reg_count)
            for j in range(radix - 1, 0, -1)
        ]
        summed = parts[:, 0].reshape((-1,) + row)

    if is_power_of_two(ep_count):
        tau_received = jnp.zeros_like(tau_grad)
        distance = 1
        while distance < ep_count:
            if distance > 1:
                tau_grad = pl.pallas_call(
                    add_kernel,
                    out_shape=shape(tau_grad.shape, F32),
                    in_specs=[VMEM, VMEM],
                    out_specs=VMEM,
                    compiler_params=params(1),
                    cost_estimate=effort(1),
                    name="add",
                )(tau_grad, tau_received)
            tau_received = to_peer(tau_grad, distance, "ep", ep_count)
            distance *= 2
    else:
        tau_grad = lax.psum(tau_grad.astype(F32), "ep")
        tau_received = jnp.zeros_like(tau_grad)

    new_prices, price_grad, wage_grad, tau_grad = pl.pallas_call(
        functools.partial(finish_kernel, len(received)),
        out_shape=(
            shape((own,) + row, BF16),
            shape((own,) + row, F32),
            shape((own, episodes), F32),
            shape(tau_grad.shape, F32),
        ),
        in_specs=[VMEM] * (7 + len(received)),
        out_specs=(VMEM,) * 4,
        compiler_params=params(4),
        name="finish",
    )(summed, *received, io_coeffs, labor_share, logsum, elastic, tau_grad, tau_received)
    return new_prices, price_grad, wage_grad, tau_grad.reshape(own, slots, sectors)


def solution(mesh):
    return jax.shard_map(
        shards,
        mesh=mesh,
        in_specs=(
            P("reg", "ep", None),
            P("reg", "ep"),
            P("reg", None),
            P("reg", None, None),
            P("reg", None, None, None),
            P("reg", None, None),
            P(),
            P(),
            P(),
            P("reg", "ep", None),
        ),
        out_specs=(
            P("reg", "ep", None),
            P("reg", "ep", None),
            P("reg", "ep"),
            P("reg", None, None),
        ),
        check_vma=False,
    )
```

```python
import functools

import jax
import jax.numpy as jnp
from jax import lax
from jax.experimental import pallas as pl
from jax.experimental.pallas import tpu as pltpu
from jax.sharding import PartitionSpec as P

F32 = jnp.float32
BF16 = jnp.bfloat16
CONTRACT_LAST = (((1,), (1,)), ((), ()))
LOWEST = -1e30
VMEM = pl.BlockSpec(memory_space=pltpu.VMEM)
SMEM = pl.BlockSpec(memory_space=pltpu.SMEM)
HBM = pl.BlockSpec(memory_space=pltpu.HBM)


def is_power_of_two(n):
    return n & (n - 1) == 0


def peer(i, distance, n):
    return i ^ distance if is_power_of_two(n) else (i + distance) % n


def distance_of(owner, me, n):
    return owner ^ me if is_power_of_two(n) else lax.rem(owner - me + n, n)


def radices(n):
    stages = []
    if n.bit_length() % 2 == 0 and is_power_of_two(n):
        stages.append(2)
        n //= 2
    while n % 4 == 0:
        stages.append(4)
        n //= 4
    if n > 1 or not stages:
        stages.append(n)
    return stages


def from_peer(x, distance, axis, n):
    return lax.ppermute(x, axis, [(peer(i, distance, n), i) for i in range(n)])


def to_peer(x, distance, axis, n):
    return lax.ppermute(x, axis, [(i, peer(i, distance, n)) for i in range(n)])


def shape(dims, dtype):
    return jax.ShapeDtypeStruct(dims, dtype)


def params(mebibytes):
    return pltpu.CompilerParams(vmem_limit_bytes=mebibytes << 20)


def effort(size):
    return pl.CostEstimate(flops=0, bytes_accessed=size, transcendentals=0)


def in_hbm(x):
    return pltpu.with_memory_space_constraint(x, pltpu.HBM)


class Entries:
    def __init__(self, own, slots, reg_count):
        self.own, self.slots, self.reg_count = own, slots, reg_count
        self.slot_count = own * slots
        self.loaded_first = 15 * own * slots // 32
        self.dense = reg_count * own <= slots
        self.capacity = own * own if self.dense else -(-own * slots // reg_count)
        self.count = self.capacity * reg_count
        self.stride = self.count + 1
        self.columns = 2 if self.dense else 4

    def numbers(self, distances):
        return [distance * self.capacity + i for distance in distances for i in range(self.capacity)]

    def turned(self, distances):
        if not self.dense:
            return []
        return [entry for entry in self.numbers(distances) if self.importer(None, entry) < max(self.own - 1, 1)]

    def slot(self, table, entry):
        return table[entry]

    def row(self, table, entry):
        return table[self.stride + entry]

    def live(self, table, entry):
        return self.row(table, entry) < self.slot_count

    def importer(self, table, entry):
        return entry % self.capacity // self.own if self.dense else table[2 * self.stride + entry]

    def place(self, table, entry):
        return entry % self.own if self.dense else table[3 * self.stride + entry]

    def fill(self, table, found, partners, lengths, me):
        own = self.own
        for entry in range(self.stride):
            for column, value in enumerate((0, self.slot_count, own, 0)[: self.columns]):
                table[column * self.stride + entry] = value
        if not self.dense:
            for distance in range(self.reg_count):
                found[distance] = 0
        for r in range(own):
            length = lengths[me * own + r]
            for s in range(self.slots):
                partner = partners[me * own + r, s]
                distance = distance_of(lax.div(partner, own), me, self.reg_count)
                place = lax.rem(partner, own)
                slot = r * self.slots + s
                if self.dense:
                    entry = distance * self.capacity + r * own + place
                    columns = (slot, slot)
                else:
                    entry = distance * self.capacity + found[distance]
                    columns = (slot, slot, r, place)
                    found[distance] += (s < length).astype(jnp.int32)
                entry = jnp.minimum(jnp.where(s < length, entry, self.count), self.count)
                for column, value in enumerate(columns):
                    table[column * self.stride + entry] = value


def load_kernel(
    entries, me_ref, cost_ref, blocks, tau, cotangent, elasticity, partners, lengths,
    held_ref, tau_ref, cotangent_ref, elasticity_ref, cost_copy_ref, table_ref,
    partners_ref, lengths_ref, found_ref, sems,
):
    copies = [
        pltpu.make_async_copy(source, target, sems.at[i])
        for i, (source, target) in enumerate(
            (
                (partners, partners_ref),
                (lengths, lengths_ref),
                (tau, tau_ref),
                (cotangent, cotangent_ref),
                (elasticity, elasticity_ref),
                (blocks.at[pl.ds(0, entries.loaded_first)], held_ref.at[pl.ds(0, entries.loaded_first)]),
            )
        )
    ]
    for copy in copies:
        copy.start()
    cost_copy_ref[...] = cost_ref[...]
    copies[0].wait()
    copies[1].wait()
    entries.fill(table_ref, found_ref, partners_ref, lengths_ref, me_ref[0])
    for copy in copies[2:]:
        copy.wait()


def scorer(entries, numbers, table_ref, costs, held_ref, tau_ref, elasticity_ref):
    scale = -elasticity_ref[...]
    rows = [(ref, block) for ref in costs for block in range(ref.shape[0] // entries.own)]

    def score(i):
        entry = numbers[i]
        ref, block = rows[i // entries.capacity]
        slot = entries.slot(table_ref, entry)
        cost = ref[block * entries.own + entries.place(table_ref, entry)]
        landed = jnp.dot(cost, held_ref[slot], preferred_element_type=F32) + tau_ref[pl.ds(slot, 1)]
        value = scale * landed
        return jnp.where(entries.live(table_ref, entry), value, -jnp.inf) if entries.dense else value

    return score


def score_entries(
    entries, distances, table_ref, costs, held_ref, tau_ref, elasticity_ref, weights_ref, top_ref, norm_ref,
    arrive=lambda r: None,
):
    own = entries.own
    numbers = entries.numbers(distances)
    count = len(numbers)
    lowest = jnp.full(top_ref.shape[1:], LOWEST, F32)
    zero = jnp.zeros(top_ref.shape[1:], F32)
    score = scorer(entries, numbers, table_ref, costs, held_ref, tau_ref, elasticity_ref)
    if entries.dense:
        for r in range(own):
            arrive(r)
            members = [i for i in range(count) if entries.importer(table_ref, numbers[i]) == r]
            scores = [score(i) for i in members]
            top = functools.reduce(jnp.maximum, scores, lowest)
            norm = zero
            for i, value in zip(members, scores):
                weight = jnp.exp(value - top)
                weights_ref[i] = weight
                norm = norm + weight
            top_ref[r] = top
            norm_ref[r] = norm
        return
    arrive(None)
    top_ref[...] = jnp.full(top_ref.shape, LOWEST, F32)
    norm_ref[...] = jnp.zeros(norm_ref.shape, F32)
    for i in range(count):
        importer = entries.importer(table_ref, numbers[i])
        value = score(i)
        weights_ref[i] = value
        top_ref[importer] = jnp.maximum(top_ref[importer], value)
    for i in range(count):
        importer = entries.importer(table_ref, numbers[i])
        weight = jnp.exp(weights_ref[i] - top_ref[importer])
        weights_ref[i] = weight
        norm_ref[importer] += weight


def near_kernel(entries, distances, turned, n_costs, *refs):
    table_ref, blocks, _, tau_ref, elasticity_ref = refs[:5]
    costs = refs[5 : 5 + n_costs]
    held_ref, weights_ref, top_ref, norm_ref, turned_ref, sems = refs[5 + n_costs :]
    copies = []
    for r in range(entries.own):
        start, stop = max(r * entries.slots, entries.loaded_first), (r + 1) * entries.slots
        if start < stop:
            part = pl.ds(start, stop - start)
            copies.append(pltpu.make_async_copy(blocks.at[part], held_ref.at[part], sems.at[r]))
    for copy in copies:
        copy.start()
    skipped = entries.own - len(copies)

    def arrive(r):
        for copy in copies if r is None else copies[r - skipped : r - skipped + 1] if r >= skipped else []:
            copy.wait()
        for i, entry in enumerate(turned):
            if r is None or entries.importer(table_ref, entry) == r:
                turned_ref[i] = held_ref[entries.slot(table_ref, entry)].T

    score_entries(
        entries, distances, table_ref, costs, held_ref, tau_ref, elasticity_ref, weights_ref, top_ref, norm_ref, arrive
    )


def push_entries(entries, distances, table_ref, adjoint_of, held_ref, total_ref, turned_ref):
    own, capacity = entries.own, entries.capacity

    def pushed(entry):
        if entry in turned:
            return jnp.dot(adjoint_of(entry), turned_ref[turned.index(entry)], preferred_element_type=F32)
        return lax.dot_general(
            adjoint_of(entry),
            held_ref[entries.slot(table_ref, entry)],
            CONTRACT_LAST,
            preferred_element_type=F32,
        )

    turned = []
    if entries.dense:
        turned = [entry for entry in entries.numbers(distances) if entries.importer(None, entry) < own // 2]
        for block, distance in enumerate(distances):
            for place in range(own):
                for r in range(own // 2):
                    entry = distance * capacity + r * own + place
                    turned_ref[turned.index(entry)] = held_ref[entries.slot(table_ref, entry)].T
                terms = [pushed(distance * capacity + r * own + place) for r in range(own)]
                total_ref[block * own + place] = sum(terms[1:], terms[0]).astype(total_ref.dtype)
        return
    total_ref[...] = jnp.zeros(total_ref.shape, total_ref.dtype)
    for block, distance in enumerate(distances):
        for entry in range(distance * capacity, (distance + 1) * capacity):
            total_ref[block * own + entries.place(table_ref, entry)] += pushed(entry)


def adjoint_kernel(entries, near_distances, far_distances, group, turned, *refs):
    table_ref, held_ref, turned_ref, tau_ref, elasticity_ref, cotangent_ref, near_weights, near_top, near_norm = refs[:9]
    costs = refs[9:-11]
    adjoint_ref, tau_grad_ref, logsum_ref, partial_ref = refs[-11:-7]
    far_weights, far_top, far_norm, factor_ref, tau_rows_ref, total_ref, late_ref = refs[-7:]
    late = [entry for entry in entries.numbers(group) if entry not in turned] if entries.dense else []
    own, capacity = entries.own, entries.capacity
    near, far = entries.numbers(near_distances), entries.numbers(far_distances)
    tau_rows_ref[...] = jnp.zeros(tau_rows_ref.shape, F32)

    def rounded(entry, value):
        tau_rows_ref[pl.ds(entries.row(table_ref, entry), 1)] = jnp.sum(value, axis=0, keepdims=True)
        return value.astype(BF16)

    def pushed(entry, value):
        if entry in turned:
            return jnp.dot(value, turned_ref[turned.index(entry)], preferred_element_type=F32)
        if entry in late:
            return jnp.dot(value, late_ref[late.index(entry)], preferred_element_type=F32)
        return lax.dot_general(
            value, held_ref[entries.slot(table_ref, entry)], CONTRACT_LAST, preferred_element_type=F32
        )

    if entries.dense:
        score = scorer(entries, far, table_ref, costs, held_ref, tau_ref, elasticity_ref)
        members = [[i for i, entry in enumerate(far) if entries.importer(None, entry) == r] for r in range(own)]

        def emit(r, entry, value):
            value = rounded(entry, value)
            if entry // capacity not in group:
                adjoint_ref[entry] = value
                return
            place = group.index(entry // capacity) * own + entries.place(None, entry)
            term = pushed(entry, value)
            total_ref[place] = term if r == 0 else total_ref[place] + term

        for r in range(own + 1):
            if r < own:
                for i in members[r]:
                    far_weights[i] = score(i)
                for i, entry in enumerate(late):
                    if r == own // 2:
                        late_ref[i] = held_ref[entries.slot(table_ref, entry)].T
            if r == 0:
                continue
            q = r - 1
            top = functools.reduce(jnp.maximum, [far_weights[i] for i in members[q]], near_top[q])
            weights = [jnp.exp(far_weights[i] - top) for i in members[q]]
            shrink = jnp.exp(near_top[q] - top)
            norm = sum(weights, near_norm[q] * shrink)
            logsum_ref[q] = top + jnp.log(norm)
            scale = cotangent_ref[q] / norm
            for i, weight in zip(members[q], weights):
                emit(q, far[i], scale * weight)
            scale = scale * shrink
            for i, entry in enumerate(near):
                if entries.importer(None, entry) == q:
                    emit(q, entry, scale * near_weights[i])
    else:
        score_entries(
            entries, far_distances, table_ref, costs, held_ref, tau_ref, elasticity_ref, far_weights, far_top, far_norm
        )
        for r in range(own):
            top = jnp.maximum(near_top[r], far_top[r])
            shrink = [jnp.exp(near_top[r] - top), jnp.exp(far_top[r] - top)]
            norm = near_norm[r] * shrink[0] + far_norm[r] * shrink[1]
            logsum_ref[r] = top + jnp.log(norm)
            for k in range(2):
                factor_ref[k, r] = cotangent_ref[r] / norm * shrink[k]
        for k in range(2):
            factor_ref[k, own] = jnp.zeros(factor_ref.shape[2:], F32)
        total_ref[...] = jnp.zeros(total_ref.shape, F32)
        for k, (numbers, weights_ref) in enumerate(((near, near_weights), (far, far_weights))):
            for i, entry in enumerate(numbers):
                value = rounded(entry, factor_ref[k, entries.importer(table_ref, entry)] * weights_ref[i])
                if entry // capacity in group:
                    place = group.index(entry // capacity) * own + entries.place(table_ref, entry)
                    total_ref[place] += pushed(entry, value)
                else:
                    adjoint_ref[entry] = value
    partial_ref[...] = total_ref[...].astype(BF16)
    tau_grad_ref[...] = tau_rows_ref[pl.ds(0, entries.slot_count)].astype(tau_grad_ref.dtype)


def push_kernel(entries, distances, table_ref, held_ref, adjoint_ref, partial_ref, total_ref, turned_ref):
    push_entries(entries, distances, table_ref, lambda entry: adjoint_ref[entry], held_ref, total_ref, turned_ref)
    partial_ref[...] = total_ref[...].astype(partial_ref.dtype)


def add_kernel(x_ref, y_ref, out_ref):
    out_ref[...] = (x_ref[...].astype(F32) + y_ref[...].astype(F32)).astype(out_ref.dtype)


def finish_kernel(n, *refs):
    own_sum_ref, received = refs[0], refs[1 : 1 + n]
    io_ref, share_ref, logsum_ref, elasticity_ref, tau_ref, tau_received_ref = refs[1 + n : 7 + n]
    prices_ref, price_grad_ref, wage_grad_ref, tau_grad_ref = refs[7 + n :]
    tau_grad_ref[...] = tau_ref[...].astype(F32) + tau_received_ref[...].astype(F32)
    for r in range(own_sum_ref.shape[0]):
        prices_ref[r] = (-logsum_ref[r] / elasticity_ref[...]).astype(BF16)
        cost_adjoint = own_sum_ref[r]
        for ref in received:
            cost_adjoint = cost_adjoint + ref[r].astype(F32)
        price_grad_ref[r] = lax.dot_general(
            cost_adjoint.astype(BF16), io_ref[r], CONTRACT_LAST, preferred_element_type=F32
        )
        wage_grad_ref[r] = jnp.sum(cost_adjoint * share_ref[pl.ds(r, 1)], axis=1)


def shards(
    log_prices,
    log_wages,
    labor_share,
    io_coeffs,
    pair_blocks,
    log_tau,
    elasticity,
    partners,
    list_lengths,
    price_cotangent,
):
    own, episodes, sectors = log_prices.shape
    slots = pair_blocks.shape[1]
    reg_count = lax.axis_size("reg")
    ep_count = lax.axis_size("ep")
    entries = Entries(own, slots, reg_count)
    blocks = pair_blocks.reshape(own * slots, sectors, sectors)
    row = (episodes, sectors)
    stages = radices(reg_count)

    unit_cost = (
        labor_share[:, None, :] * log_wages[:, :, None]
        + jnp.einsum("iek,ikj->iej", log_prices, io_coeffs, preferred_element_type=F32)
    ).astype(BF16)

    held, tau, cotangent, elastic, cost_copy, table = pl.pallas_call(
        functools.partial(load_kernel, entries),
        out_shape=(
            shape(blocks.shape, BF16),
            shape((own * slots, sectors), F32),
            shape(price_cotangent.shape, F32),
            shape((1, sectors), F32),
            shape(unit_cost.shape, BF16),
            pltpu.SMEM((entries.columns * entries.stride,), jnp.int32),
        ),
        in_specs=[SMEM, VMEM] + [HBM] * 6,
        out_specs=(VMEM,) * 5 + (SMEM,),
        scratch_shapes=[
            pltpu.SMEM(partners.shape, jnp.int32),
            pltpu.SMEM(list_lengths.shape, jnp.int32),
            pltpu.SMEM((reg_count,), jnp.int32),
            pltpu.SemaphoreType.DMA((6,)),
        ],
        compiler_params=params(1),
        cost_estimate=effort(blocks.size),
        name="load",
    )(
        lax.axis_index("reg").reshape(1),
        unit_cost,
        in_hbm(blocks),
        in_hbm(log_tau.reshape(own * slots, sectors)),
        in_hbm(price_cotangent),
        in_hbm(elasticity.reshape(1, sectors)),
        in_hbm(partners),
        in_hbm(list_lengths),
    )

    near, near_distances = [unit_cost], [0]
    stride = reg_count
    for radix in reversed(stages):
        stride //= radix
        whole, distances = jnp.concatenate(near, axis=0), near_distances
        order = [*range(2, radix), 1]
        received = [from_peer(whole, j * stride, "reg", reg_count) for j in order]
        reached = [[d + j * stride for d in distances] for j in order]
        near[0] = cost_copy
        if stride > 1:
            near = near + received
            near_distances = sum(reached, distances)
    far_distances = sum(reached, [])

    def scored(distances):
        return (
            shape((len(distances) * entries.capacity,) + row, F32),
            shape((own + 1,) + row, F32),
            shape((own + 1,) + row, F32),
        )

    radix = stages[0]
    groups = [range(j, reg_count, radix) for j in range(radix)]
    turned = entries.turned(groups[-1])
    held, *near_scores, turned_blocks = pl.pallas_call(
        functools.partial(near_kernel, entries, near_distances, turned, len(near)),
        out_shape=(shape(blocks.shape, BF16),)
        + scored(near_distances)
        + (shape((max(len(turned), 1), sectors, sectors), BF16),),
        in_specs=[SMEM, HBM] + [VMEM] * (3 + len(near)),
        out_specs=(VMEM,) * 5,
        scratch_shapes=[pltpu.SemaphoreType.DMA((own,))],
        input_output_aliases={2: 0},
        compiler_params=params(2),
        cost_estimate=effort(blocks.size),
        name="near",
    )(table, in_hbm(blocks), held, tau, elastic, *near)
    partial_dims = (reg_count // radix * own,) + row
    adjoint, tau_grad, logsum, partial = pl.pallas_call(
        functools.partial(adjoint_kernel, entries, near_distances, far_distances, groups[-1], turned),
        out_shape=(
            shape((entries.count,) + row, BF16),
            shape((own * slots, sectors), BF16),
            shape((own,) + row, F32),
            shape(partial_dims, BF16),
        ),
        in_specs=[SMEM] + [VMEM] * (8 + len(received)),
        out_specs=(VMEM,) * 4,
        scratch_shapes=[
            *[pltpu.VMEM(s.shape, F32) for s in scored(far_distances)],
            pltpu.VMEM((2, own + 1) + row, F32),
            pltpu.VMEM((own * slots + 8, sectors), F32),
            pltpu.VMEM(partial_dims, F32),
            pltpu.VMEM((max((len(groups[-1]) * entries.capacity - len(turned)) * entries.dense, 1), sectors, sectors), BF16),
        ],
        compiler_params=params(16),
        cost_estimate=effort(blocks.size),
        name="adjoint",
    )(table, held, turned_blocks, tau, elastic, cotangent, *near_scores, *received)

    def push(j, dtype):
        return pl.pallas_call(
            functools.partial(push_kernel, entries, groups[j]),
            out_shape=shape(partial_dims, dtype),
            in_specs=[SMEM, VMEM, VMEM],
            out_specs=VMEM,
            scratch_shapes=[
                pltpu.VMEM(partial_dims, F32),
                pltpu.VMEM((max(len(groups[j]) * own * (own // 2) * entries.dense, 1), sectors, sectors), BF16),
            ],
            compiler_params=params(16),
            cost_estimate=effort(blocks.size),
            name="push",
        )(table, held, adjoint)

    received = [to_peer(partial, radix - 1, "reg", reg_count)] if radix > 1 else []
    for j in range(radix - 2, 0, -1):
        received.append(to_peer(push(j, BF16), j, "reg", reg_count))
    summed = push(0, F32) if radix > 1 else partial.astype(F32)
    stride = 1
    for following in stages[1:]:
        for block in received:
            summed = summed + block.astype(F32)
        stride *= radix
        radix = following
        parts = summed.reshape((-1, radix, own) + row)
        received = [
            to_peer(parts[:, j].reshape((-1,) + row).astype(BF16), j * stride, "reg", reg_count)
            for j in range(radix - 1, 0, -1)
        ]
        summed = parts[:, 0].reshape((-1,) + row)

    if is_power_of_two(ep_count):
        tau_received = jnp.zeros_like(tau_grad)
        distance = 1
        while distance < ep_count:
            if distance > 1:
                tau_grad = pl.pallas_call(
                    add_kernel,
                    out_shape=shape(tau_grad.shape, F32),
                    in_specs=[VMEM, VMEM],
                    out_specs=VMEM,
                    compiler_params=params(1),
                    cost_estimate=effort(1),
                    name="add",
                )(tau_grad, tau_received)
            tau_received = to_peer(tau_grad, distance, "ep", ep_count)
            distance *= 2
    else:
        tau_grad = lax.psum(tau_grad.astype(F32), "ep")
        tau_received = jnp.zeros_like(tau_grad)

    new_prices, price_grad, wage_grad, tau_grad = pl.pallas_call(
        functools.partial(finish_kernel, len(received)),
        out_shape=(
            shape((own,) + row, BF16),
            shape((own,) + row, F32),
            shape((own, episodes), F32),
            shape(tau_grad.shape, F32),
        ),
        in_specs=[VMEM] * (7 + len(received)),
        out_specs=(VMEM,) * 4,
        compiler_params=params(4),
        name="finish",
    )(summed, *received, io_coeffs, labor_share, logsum, elastic, tau_grad, tau_received)
    return new_prices, price_grad, wage_grad, tau_grad.reshape(own, slots, sectors)


def solution(mesh):
    return jax.shard_map(
        shards,
        mesh=mesh,
        in_specs=(
            P("reg", "ep", None),
            P("reg", "ep"),
            P("reg", None),
            P("reg", None, None),
            P("reg", None, None, None),
            P("reg", None, None),
            P(),
            P(),
            P(),
            P("reg", "ep", None),
        ),
        out_specs=(
            P("reg", "ep", None),
            P("reg", "ep", None),
            P("reg", "ep"),
            P("reg", None, None),
        ),
        check_vma=False,
    )
```
